256 devices in a mesh: tile: 16 (over y, z_lo, core), seq: 16 (over x, z_hi).
Axes of the slice: x: 4, y: 4, z: 8 (z_hi: 4, z_lo: 2; z = z_hi * 2 + z_lo), core: 2. Of those that a mesh axis runs over, the one named last changes fastest.
Arguments:
- scene_band: bfloat16 [32, 1536, 768], P('seq', 'tile'), may hold values from -6 to 6
- tile_list: int32 [16, 3], replicated, may hold values from 0 to 32, as said below
- embed_weight: bfloat16 [768, 1024], replicated, may hold values from -0.21875 to 0.21875
- position: bfloat16 [2048, 1024], P('seq'), may hold values from -3 to 3
- norm_gains: float32 [3, 1024], replicated, may hold values from 0.1 to 1.9
- window_qkv: bfloat16 [1024, 3072], replicated
- window_out: bfloat16 [1024, 1024], replicated, may hold values from -0.1875 to 0.1875
- global_qkv: bfloat16 [1024, 3072], P(None, 'seq')
- global_out: bfloat16 [1024, 1024], P('seq')
- head_weight: bfloat16 [1024, 128], replicated, may hold values from -0.1875 to 0.1875
Outputs:
- strip_logits: float32 [32, 1536, 128], P('seq', 'tile')
The draws below stay inside these ranges and needn't reach their ends.
Inputs may be any that keep to these rules, and one draw needn't show every extreme that they name: `tile_list`: column 0 is a tile's owning strip, 0 to 15; no strip owns more than 3 tiles and one strip owns exactly 3. Column 1 is the offset, 0 to 32, reached by some tile; column 2 the zero columns before the tile, 0 to 15, reached by some tile.
All inputs are finite; a program needn't handle non-finite values.
Results may differ from the reference program's by a relative error of at most 0.024.
Values may be sent and summed in bfloat16 or wider, within the bound.
A program may use at most 192 MiB of HBM per device.

```python
import math
import jax
import jax.numpy as jnp
from jax import lax

D = 1024
H = 16
HD = 64
PV = 768
NCLS = 128
TC = 64
WIN = 16
SC = 96
PADMAX = 16
MOST = 3
TILES = 16
TR = 32
TILE_TOK = 2048
MOS_C = 1536


def draw_tile_list(key, part):
    key = jax.random.fold_in(key, 11)
    keys = jax.random.split(key, 5)
    chosen_strip = jax.random.randint(keys[0], (), 0, TILES)
    slot_order = jax.random.permutation(keys[1], TILES * MOST)
    slot_strip = slot_order // MOST
    ranking = jnp.where(slot_strip == chosen_strip, -1, jnp.arange(TILES * MOST))
    picked = slot_order[jnp.argsort(ranking, stable=True)[:TILES]]
    owners = (picked // MOST)[jax.random.permutation(keys[2], TILES)]
    offsets = jax.random.randint(keys[3], (TILES,), 0, SC - TC + 1).at[0].set(SC - TC)
    zeros_before = jax.random.randint(keys[4], (TILES,), 0, PADMAX).at[TILES - 1].set(PADMAX - 1)
    return jnp.stack([owners, offsets, zeros_before], axis=1).astype(jnp.int32)


def draw_window_qkv(key, part):
    key = jax.random.fold_in(key, 23)
    base = jax.random.normal(key, (D, H, 3, HD), jnp.float32) * D ** (-0.5)
    return base.reshape(D, 3 * D).astype(jnp.bfloat16)


def draw_global_qkv(key, part):
    key = jax.random.fold_in(key, 37)
    base = jax.random.normal(key, (D, H, 3, HD), jnp.float32) * D ** (-0.5)
    return base.reshape(D, 3 * D).astype(jnp.bfloat16)


def draw_global_out(key, part):
    key = jax.random.fold_in(key, 41)
    scale = math.sqrt(TILE_TOK / D)
    base = jnp.clip(jax.random.normal(key, (D, D), jnp.float32), -6.0, 6.0) * scale
    return base.astype(jnp.bfloat16)


def block_levels(own_key, shape, cuts, least, high):
    factor_of = 1.0
    for dim, blocks in cuts:
        draws = jax.random.uniform(jax.random.fold_in(jax.random.fold_in(own_key, 6), dim), (blocks,), jnp.float32, least / len(cuts), high / len(cuts))
        factor_of = factor_of * jnp.repeat(jnp.exp(draws), shape[dim] // blocks).reshape((-1,) + (1,) * (len(shape) - 1 - dim))
    return factor_of


def bell_draw(stream_key, dims, scale, bound, cuts=(), kind=jnp.bfloat16):
    result = jax.random.normal(stream_key, dims, jnp.float32) * scale
    if len(cuts) > 0:
        result = block_levels(stream_key, dims, cuts, -0.22, 0.18) * result
    return jnp.clip(result, min=-bound, max=bound).astype(kind)


def setup_inputs(seed: int = 0) -> dict:
    arg_keys = jax.random.split(jax.random.key(seed), 11)
    return {
        "scene_band": bell_draw(arg_keys[0], (TR, MOS_C, PV), 1.0, 6.0, ((0, 16), (1, 16))),
        "tile_list": draw_tile_list(jax.random.fold_in(arg_keys[10], 71), 0),
        "embed_weight": bell_draw(arg_keys[2], (PV, D), PV ** -0.5, 0.21875),
        "position": bell_draw(arg_keys[3], (TILE_TOK, D), 0.5, 3.0, ((0, 16),)),
        "norm_gains": jnp.clip(1.0 + 0.18 * jax.random.normal(arg_keys[4], (3, D), jnp.float32), 0.1, 1.9),
        "window_qkv": draw_window_qkv(jax.random.fold_in(arg_keys[10], 71), 0),
        "window_out": bell_draw(arg_keys[6], (D, D), D ** -0.5, 0.1875),
        "global_qkv": draw_global_qkv(jax.random.fold_in(arg_keys[10], 71), 0),
        "global_out": draw_global_out(jax.random.fold_in(arg_keys[10], 71), 0),
        "head_weight": bell_draw(arg_keys[9], (D, NCLS), D ** -0.5, 0.1875),
    }


EPSILON = 1e-06

def layer_norm(stream, gain):
    centre = stream - lax.optimization_barrier(jnp.mean(stream, axis=-1, keepdims=True))
    spread = lax.optimization_barrier(jnp.mean(centre * centre, axis=-1, keepdims=True))
    return (centre * lax.rsqrt(spread + EPSILON) * gain).astype(jnp.bfloat16)

def attend(queries, keys, values):
    scores = jnp.einsum('qhd,khd->hqk', queries.astype(jnp.float32), keys.astype(jnp.float32)) * HD ** (-0.5)
    weights = jax.nn.softmax(scores, axis=-1).astype(jnp.bfloat16)
    return jnp.einsum('hqk,khd->qhd', weights.astype(jnp.float32), values.astype(jnp.float32)).astype(jnp.bfloat16)

def window_block(stream, gain, qkv_weight, out_weight):
    normed = layer_norm(stream, gain)
    projected = jnp.dot(normed, qkv_weight, preferred_element_type=jnp.float32).astype(jnp.bfloat16)
    grouped = projected.reshape(TR // WIN, WIN, TC // WIN, WIN, H, 3, HD).transpose(0, 2, 1, 3, 4, 5, 6)
    grouped = grouped.reshape(TR // WIN * (TC // WIN), WIN * WIN, H, 3, HD)
    mixed = lax.map(lambda group: attend(group[:, :, 0], group[:, :, 1], group[:, :, 2]), grouped)
    mixed = mixed.reshape(TR // WIN, TC // WIN, WIN, WIN, D).transpose(0, 2, 1, 3, 4).reshape(TILE_TOK, D)
    return stream + jnp.dot(mixed, out_weight, preferred_element_type=jnp.float32)

def global_block(stream, gain, qkv_weight, out_weight):
    normed = layer_norm(stream, gain)
    projected = jnp.dot(normed, qkv_weight, preferred_element_type=jnp.float32).astype(jnp.bfloat16)
    by_head = projected.reshape(TILE_TOK, H, 3, HD).transpose(1, 0, 2, 3)
    mixed = lax.map(lambda single: attend(single[:, None, 0], single[:, None, 1], single[:, None, 2])[:, 0], by_head)
    mixed = mixed.transpose(1, 0, 2).reshape(TILE_TOK, D)
    return stream + jnp.dot(mixed, out_weight, preferred_element_type=jnp.float32)

def reference(scene_band, tile_list, embed_weight, position, norm_gains, window_qkv, window_out, global_qkv, global_out, head_weight):
    owners = tile_list[:, 0].astype(jnp.int32)
    starts = (tile_list[:, 1] - tile_list[:, 2] + PADMAX).astype(jnp.int32)
    strips = scene_band.reshape(TR, TILES, SC, PV)
    padded = jnp.concatenate([jnp.zeros((TR, TILES, PADMAX, PV), scene_band.dtype), strips], axis=2)
    zero_index = jnp.zeros((), jnp.int32)

    def one_tile(index):
        corner = (zero_index, owners[index], starts[index], zero_index)
        block = lax.dynamic_slice(padded, corner, (TR, 1, TC, PV)).reshape(TILE_TOK, PV)
        stream = jnp.dot(block, embed_weight, preferred_element_type=jnp.float32) + position.astype(jnp.float32)
        stream = window_block(stream, norm_gains[0], window_qkv, window_out)
        stream = global_block(stream, norm_gains[1], global_qkv, global_out)
        return jnp.dot(layer_norm(stream, norm_gains[2]), head_weight, preferred_element_type=jnp.float32)
    logits = lax.map(one_tile, jnp.arange(TILES, dtype=jnp.int32))
    totals = jnp.zeros((TILES, TR, PADMAX + SC, NCLS), jnp.float32)
    counts = jnp.zeros((TILES, PADMAX + SC), jnp.float32)
    columns = jnp.arange(PADMAX + SC, dtype=jnp.int32)
    strip_ids = jnp.arange(TILES, dtype=jnp.int32)
    for index in range(TILES):
        tile_block = logits[index].reshape(1, TR, TC, NCLS)
        corner = (owners[index], zero_index, starts[index], zero_index)
        current = lax.dynamic_slice(totals, corner, (1, TR, TC, NCLS))
        totals = lax.dynamic_update_slice(totals, current + tile_block, corner)
        cover = ((columns >= starts[index]) & (columns < starts[index] + TC)).astype(jnp.float32)
        counts = counts + (strip_ids[:, None] == owners[index]).astype(jnp.float32) * cover[None, :]
    averaged = totals[:, :, PADMAX:] / jnp.maximum(counts[:, PADMAX:], 1.0)[:, None, :, None]
    return averaged.transpose(1, 0, 2, 3).reshape(TR, TILES * SC, NCLS)
```

```python
import functools
import jax
import jax.numpy as jnp
from jax import lax
from jax.experimental import pallas as pl
from jax.experimental.pallas import tpu as pltpu
from jax.sharding import PartitionSpec as P

D = 1024
HD = 64
PADMAX = 16
MOST = 3
N = 16
SC = 96
PV = 768
FH = 384
NCLS = 128
EPSILON = 1e-06
FAR = 4096
NT = (((1,), (1,)), ((), ()))


def layer_norm(stream, gain):
    centre = stream - jnp.mean(stream, axis=-1, keepdims=True)
    spread = jnp.mean(centre * centre, axis=-1, keepdims=True)
    return (centre * lax.rsqrt(spread + EPSILON) * gain).astype(jnp.bfloat16)


def dot(a, b):
    return jnp.dot(a, b, preferred_element_type=jnp.float32)


def remote(src, dst, send_sem, recv_sem, tile, seq):
    return pltpu.make_async_remote_copy(
        src_ref=src, dst_ref=dst, send_sem=send_sem, recv_sem=recv_sem,
        device_id=(tile, seq), device_id_type=pl.DeviceIdType.MESH,
    )


def loop(low, high, body):
    def step(k, carry):
        body(k)
        return carry

    lax.fori_loop(low, high, step, 0)


def kernel(
    tl, strip, pos, wq, wo, gains, we_hbm, w1_hbm, wout_hbm, hw_hbm, out_ref,
    we, w1, wout, hw, load_sem,
    out1, in1, fwd, pix, posall, nbuf, x_ref, o1,
    wqall, woall, q_out, q_in, qt, kb, vt, o_out, o_in,
    lout, lin, rout, rin,
    entered,
    p1s, p1r, p2s, p2r, pos_s, pos_r, sib_s, sib_r,
    qzs, qxs, qss, qr, qsr, ozs, oxs, oss, orr, osr,
    as_, ar, bs, br, l1s, l1r, l2s, l2r,
):
    i = lax.axis_index("tile")
    r = lax.axis_index("seq")
    core = i % 2
    sibling = i + 1 - 2 * core
    x_at = r // 4
    z_at = r % 4
    band = i // 4
    upper = (i % 4) // 2
    kc_mine = 2 * band + core
    r8 = r // 8
    rm = r % 8

    loads = [
        pltpu.make_async_copy(we_hbm, we, load_sem.at[0]),
        pltpu.make_async_copy(w1_hbm, w1, load_sem.at[1]),
        pltpu.make_async_copy(wout_hbm, wout, load_sem.at[2]),
        pltpu.make_async_copy(hw_hbm, hw, load_sem.at[3]),
    ]
    for load in loads:
        load.start()

    barrier = pltpu.get_barrier_semaphore()

    def greet(k):
        pl.semaphore_signal(
            barrier, inc=1, device_id=((i + k) % N, r), device_id_type=pl.DeviceIdType.MESH
        )
        pl.semaphore_signal(
            barrier, inc=1, device_id=(i, (r + k) % N), device_id_type=pl.DeviceIdType.MESH
        )

    loop(1, N, greet)

    owners = [tl[t, 0] for t in range(N)]
    starts = [tl[t, 1] - tl[t, 2] for t in range(N)]
    ranks = []
    for t in range(N):
        rank = jnp.int32(0)
        for u in range(t):
            rank = rank + jnp.where(owners[u] == owners[t], 1, 0)
        ranks.append(jnp.minimum(rank, MOST - 1))
    begin = []
    for m in range(MOST):
        value = jnp.int32(FAR)
        for t in range(N):
            value = jnp.where((owners[t] == i) & (ranks[t] == m), starts[t], value)
        begin.append(value)

    cells = strip[...].reshape(2 * SC, PV)
    token = lax.broadcasted_iota(jnp.int32, (128, 2 * SC), 0)
    cell = lax.broadcasted_iota(jnp.int32, (128, 2 * SC), 1)
    t_row = (token // 8) % 2
    t_col = (token // 16) * 8 + token % 8
    c_row = jnp.where(cell >= SC, 1, 0)
    c_col = cell - SC * c_row
    for m in range(MOST):
        chosen = (c_row == t_row) & (c_col == t_col + begin[m])
        block = dot(jnp.where(chosen, 1.0, 0.0).astype(jnp.bfloat16), cells).astype(jnp.bfloat16)
        for c in range(N):
            k, f = c // 2, c % 2
            out1[c, m] = block[k * 16 : k * 16 + 16, f * FH : f * FH + FH]

    pl.semaphore_wait(barrier, 2 * (N - 1))

    def p1(c):
        return remote(out1.at[c], in1.at[i], p1s.at[c], p1r.at[i], c, r)

    def p1_in(s):
        return remote(out1.at[s], in1.at[s], p1s.at[s], p1r.at[s], s, r)

    loop(1, N, lambda k: p1((i + k) % N).start())
    in1[i] = out1[i]

    def greet_again(k):
        pl.semaphore_signal(
            entered, inc=1, device_id=(i, (r + k) % N), device_id_type=pl.DeviceIdType.MESH
        )

    loop(1, N, greet_again)

    def pos_copy(t):
        return remote(pos, posall.at[rm], pos_s.at[t], pos_r.at[rm], i, t)

    @pl.when(upper == r8)
    def _():
        loop(1, N, lambda k: pos_copy((r + k) % N).start())
        posall[rm] = pos[...]

    def along_z(src, full, zs, got, k):
        return remote(
            src.at[core], full.at[r, core], zs.at[k - 1], got.at[r], i, x_at * 4 + (z_at + k) % 4
        )

    def along_x(src, full, xs, got, z, k):
        shard = x_at * 4 + z
        piece = src.at[core] if src is not None else full.at[shard, core]
        return remote(
            piece, full.at[shard, core], xs.at[z * 3 + k - 1], got.at[shard],
            i, ((x_at + k) % 4) * 4 + z_at,
        )

    def arrival(src, full, zs, got, shard):
        return remote(src.at[core], full.at[shard, core], zs.at[0], got.at[shard], i, r)

    def to_sibling(full, ss, got, shard):
        return remote(
            full.at[shard, core], full.at[shard, core], ss.at[shard], got.at[shard], sibling, r
        )

    def from_sibling(full, ss, got, shard):
        return remote(
            full.at[shard, 1 - core], full.at[shard, 1 - core], ss.at[shard], got.at[shard],
            sibling, r,
        )

    def spread_own(src, full, zs, xs, got):
        for k in range(1, 4):
            along_z(src, full, zs, got, k).start()
        for k in range(1, 4):
            along_x(src, full, xs, got, z_at, k).start()
        full[r] = src[...]

    def pass_z(src, full, zs, xs, ss, got, sgot):
        def one(k):
            z = (z_at + k) % 4
            arrival(src, full, zs, got, x_at * 4 + z).wait_recv()
            for d in range(1, 4):
                along_x(None, full, xs, got, z, d).start()
            to_sibling(full, ss, sgot, x_at * 4 + z).start()

        loop(1, 4, one)

    def pass_x(src, full, zs, ss, got, sgot, k):
        z = (z_at + k) % 4
        for d in range(1, 4):
            shard = ((x_at + d) % 4) * 4 + z
            arrival(src, full, zs, got, shard).wait_recv()
            to_sibling(full, ss, sgot, shard).start()

    def finish_sends(src, full, zs, xs, ss, got, sgot):
        for k in range(1, 4):
            along_z(src, full, zs, got, k).wait_send()
        for k in range(0, 4):
            for d in range(1, 4):
                along_x(None, full, xs, got, (z_at + k) % 4, d).wait_send()

        loop(1, N, lambda k: to_sibling(full, ss, sgot, (r + k) % N).wait_send())

    spread_own(wq, wqall, qzs, qxs, qr)

    loop(1, N, lambda k: p1_in((i + k) % N).wait_recv())
    for t in range(N):
        fwd[t] = in1[owners[t], ranks[t]]
    pl.semaphore_wait(entered, N - 1)

    half_c = (i % 4) // 2
    worker = band * 4 + r8 * 2 + half_c

    def p2(t):
        return remote(
            fwd.at[t], pix.at[core, rm], p2s.at[t], p2r.at[core * 8 + rm], worker, t
        )

    loop(1, N, lambda k: p2((r + k) % N).start())

    @pl.when(worker != i)
    def _():
        p2(r).start()

    @pl.when(worker == i)
    def _():
        pix[core, rm] = fwd[r]

    pass_z(wq, wqall, qzs, qxs, qss, qr, qsr)

    for f in range(2):
        source = band * 4 + core * 2 + f

        def p2_in(k, f=f, source=source):
            @pl.when((source != i) | (upper * 8 + k != r))
            def _():
                remote(
                    fwd.at[0], pix.at[f, k], p2s.at[0], p2r.at[f * 8 + k], i, r
                ).wait_recv()

        loop(0, 8, p2_in)

    def pos_in(k):
        @pl.when(upper * 8 + k != r)
        def _():
            remote(pos, posall.at[k], pos_s.at[0], pos_r.at[k], i, r).wait_recv()

    loop(0, 8, pos_in)
    loads[0].wait()
    stream = dot(pix[0].reshape(128, FH), we[0:FH]) + dot(pix[1].reshape(128, FH), we[FH:PV])
    stream = stream + posall[...].reshape(128, D).astype(jnp.float32)
    x_ref[...] = stream
    nbuf[core] = layer_norm(stream, gains[0:1])
    sib = remote(nbuf.at[core], nbuf.at[core], sib_s, sib_r, sibling, r)
    sib.start()
    sib_in = remote(nbuf.at[1 - core], nbuf.at[1 - core], sib_s, sib_r, sibling, r)
    loads[1].wait()
    sib_in.wait_recv()

    def window_heads(pair):
        columns = w1[:, pl.ds(pl.multiple_of(pair * 384, 384), 384)]
        mine = dot(nbuf[core], columns).astype(jnp.bfloat16)
        other = dot(nbuf[1 - core], columns).astype(jnp.bfloat16)
        both = jnp.concatenate([mine, other], axis=0)
        results = []
        for h in range(2):
            at = h * 192
            scores = lax.dot_general(
                mine[:, at : at + 64], both[:, at + 64 : at + 128], NT,
                preferred_element_type=jnp.float32,
            ) * HD ** (-0.5)
            top = jnp.max(scores, axis=-1, keepdims=True)
            weights = jnp.exp(scores - top)
            weights = weights / jnp.sum(weights, axis=-1, keepdims=True)
            results.append(dot(weights.astype(jnp.bfloat16), both[:, at + 128 : at + 192]))
        o1[:, pl.ds(pl.multiple_of(pair * 128, 128), 128)] = jnp.concatenate(
            results, axis=1
        ).astype(jnp.bfloat16)

    loop(0, 4, window_heads)
    pass_x(wq, wqall, qzs, qss, qr, qsr, 0)
    loop(4, 8, window_heads)
    loads[2].wait()
    stream = x_ref[...] + dot(o1[...], wout[...])
    x_ref[...] = stream
    normed = layer_norm(stream, gains[1:2])
    for k in range(1, 4):
        pass_x(wq, wqall, qzs, qss, qr, qsr, k)
    loop(1, N, lambda k: from_sibling(wqall, qss, qsr, (r + k) % N).wait_recv())

    def to_head(h):
        return remote(q_out.at[h], q_in.at[i], as_.at[h], ar.at[i], h, r)

    def project(k):
        h = (i + k) % N
        q_out[h] = lax.dot_general(
            wqall[h].reshape(192, D), normed, NT, preferred_element_type=jnp.float32
        ).astype(jnp.bfloat16)
        to_head(h).start()

    loop(1, N, project)
    q_in[i] = lax.dot_general(
        wqall[i].reshape(192, D), normed, NT, preferred_element_type=jnp.float32
    ).astype(jnp.bfloat16)

    spread_own(wo, woall, ozs, oxs, orr)

    def head_in(k):
        s = (i + k) % N
        remote(q_out.at[s], q_in.at[s], as_.at[s], ar.at[s], s, r).wait_recv()

    loop(1, N, head_in)
    for s in range(N):
        at = s * 128
        qt[:, at : at + 128] = q_in[s, 0:64]
        kb[at : at + 128, :] = q_in[s, 64:128].astype(jnp.float32).T.astype(jnp.bfloat16)
        vt[:, at : at + 128] = q_in[s, 128:192]

    def home(j):
        return remote(o_out.at[j], o_in.at[i], bs.at[j], br.at[i], j, r)

    def attend(k):
        b = (k + i // 2 + 1) % 8
        queries = qt[:, pl.ds(pl.multiple_of(b * 256, 256), 256)]
        scores = dot(kb[...], queries)
        top = jnp.max(scores, axis=0, keepdims=True)
        weights = jnp.exp2((scores - top) * (HD ** (-0.5) * 1.4426950408889634))
        total = jnp.sum(weights, axis=0, keepdims=True)
        mixed = (dot(vt[...], weights.astype(jnp.bfloat16)) / total).astype(jnp.bfloat16)
        o_out[2 * b] = mixed[:, 0:128]
        o_out[2 * b + 1] = mixed[:, 128:256]
        for e in range(2):
            j = 2 * b + e

            @pl.when(j != i)
            def _(j=j):
                home(j).start()

    loop(0, 2, attend)
    pass_z(wo, woall, ozs, oxs, oss, orr, osr)
    loop(2, 7, attend)
    for k in range(0, 4):
        pass_x(wo, woall, ozs, oss, orr, osr, k)
    loop(7, 8, attend)
    o_in[i] = o_out[i]
    loop(1, N, lambda k: from_sibling(woall, oss, osr, (r + k) % N).wait_recv())

    def home_in(k):
        s = (i + k) % N
        remote(o_out.at[s], o_in.at[s], bs.at[s], br.at[s], s, r).wait_recv()

    loop(1, N, home_in)
    attended = o_in[...].reshape(D, 128).astype(jnp.float32).T.astype(jnp.bfloat16)
    stream = x_ref[...] + dot(attended, woall[...].reshape(D, D))
    loads[3].wait()
    logits = dot(layer_norm(stream, gains[2:3]), hw[...])
    lout[...] = logits.astype(jnp.bfloat16).reshape(8, 16, NCLS)

    collector = 2 * kc_mine + r % 2

    def l1(k):
        return remote(
            lout.at[k], lin.at[r // 2], l1s.at[k], l1r.at[r // 2], collector, upper * 8 + k
        )

    def l1_start(k):
        away = (collector != i) | (upper * 8 + k != r)

        @pl.when(away)
        def _():
            l1(k).start()

        @pl.when(jnp.logical_not(away))
        def _():
            lin[r // 2] = lout[k]

    loop(0, 8, l1_start)
    kc = i // 2
    giver = (kc // 2) * 4 + r8 * 2 + kc % 2

    def l1_in(k):
        @pl.when((giver != i) | (2 * k + i % 2 != r))
        def _():
            remote(lout.at[0], lin.at[k], l1s.at[0], l1r.at[k], i, r).wait_recv()

    slot = [owners[t] * MOST + ranks[t] for t in range(N)]
    lane = lax.broadcasted_iota(jnp.int32, (N * MOST * 16, 128), 1)
    line = lax.broadcasted_iota(jnp.int32, (N * MOST * 16, 128), 0)
    wanted = jnp.zeros((N * MOST * 16, 128), jnp.int32)
    for k in range(8):
        wanted = jnp.where(
            lane // 16 == k, jnp.where(core == 0, slot[2 * k], slot[2 * k + 1]), wanted
        )
    route = jnp.where(line == wanted * 16 + lane % 16, 1.0, 0.0).astype(jnp.bfloat16)
    loop(0, 8, l1_in)
    rout[...] = (
        dot(route, lin[...].reshape(128, NCLS)).astype(jnp.bfloat16).reshape(N, MOST, 16, NCLS)
    )

    def l2(s):
        return remote(rout.at[s], rin.at[i], l2s.at[s], l2r.at[i], s, r)

    loop(1, N, lambda k: l2((i + k) % N).start())
    rin[i] = rout[i]

    cell = lax.broadcasted_iota(jnp.int32, (2 * SC, 128), 0)
    token = lax.broadcasted_iota(jnp.int32, (2 * SC, 128), 1)
    t_row = (token // 8) % 2
    t_col = (token // 16) * 8 + token % 8
    c_row = jnp.where(cell >= SC, 1, 0)
    c_col = cell - SC * c_row
    count = jnp.zeros((2 * SC, 128), jnp.float32)
    spots = []
    for m in range(MOST):
        chosen = (c_row == t_row) & (c_col == t_col + begin[m])
        spots.append(jnp.where(chosen, 1.0, 0.0).astype(jnp.bfloat16))
        count = count + jnp.where((c_col >= begin[m]) & (c_col < begin[m] + 64), 1.0, 0.0)

    def l2_in(k):
        s = (i + k) % N
        remote(rout.at[s], rin.at[s], l2s.at[s], l2r.at[s], s, r).wait_recv()

    loop(1, N, l2_in)
    total = jnp.zeros((2 * SC, NCLS), jnp.float32)
    for m in range(MOST):
        pieces = [rin[2 * k, m] + rin[2 * k + 1, m] for k in range(8)]
        total = total + dot(spots[m], jnp.concatenate(pieces, axis=0))
    out_ref[...] = (total / jnp.maximum(count, 1.0)).reshape(2, SC, NCLS)

    loop(1, N, lambda k: p1((i + k) % N).wait_send())

    @pl.when(upper == r8)
    def _():
        loop(1, N, lambda k: pos_copy((r + k) % N).wait_send())

    loop(1, N, lambda k: p2((r + k) % N).wait_send())

    @pl.when(worker != i)
    def _():
        p2(r).wait_send()

    sib.wait_send()
    finish_sends(wq, wqall, qzs, qxs, qss, qr, qsr)
    finish_sends(wo, woall, ozs, oxs, oss, orr, osr)
    loop(1, N, lambda k: to_head((i + k) % N).wait_send())
    loop(1, N, lambda k: home((i + k) % N).wait_send())

    def l1_sent(k):
        @pl.when((collector != i) | (upper * 8 + k != r))
        def _():
            l1(k).wait_send()

    loop(0, 8, l1_sent)
    loop(1, N, lambda k: l2((i + k) % N).wait_send())


def local(
    scene_band, tile_list, embed_weight, position, norm_gains, window_qkv, window_out,
    global_qkv, global_out, head_weight,
):
    i = lax.axis_index("tile")
    column = 2 * (i // 4) + i % 2
    pos = lax.dynamic_slice_in_dim(position.reshape(2, 64, D), column * 8, 8, 1).reshape(16, D)
    wq = global_qkv.T.reshape(2, 96, D)
    wo = global_out.reshape(2, 32, D)
    bf = jnp.bfloat16
    vmem = pl.BlockSpec(memory_space=pltpu.VMEM)
    hbm = pl.BlockSpec(memory_space=pl.ANY)
    dma = pltpu.SemaphoreType.DMA
    return pl.pallas_call(
        kernel,
        out_shape=jax.ShapeDtypeStruct((2, SC, NCLS), jnp.float32),
        in_specs=[pl.BlockSpec(memory_space=pltpu.SMEM)] + [vmem] * 5 + [hbm] * 4,
        out_specs=vmem,
        scratch_shapes=[
            pltpu.VMEM((PV, D), bf),
            pltpu.VMEM((D, 3 * D), bf),
            pltpu.VMEM((D, D), bf),
            pltpu.VMEM((D, NCLS), bf),
            dma((4,)),
            pltpu.VMEM((N, MOST, 16, FH), bf),
            pltpu.VMEM((N, MOST, 16, FH), bf),
            pltpu.VMEM((N, 16, FH), bf),
            pltpu.VMEM((2, 8, 16, FH), bf),
            pltpu.VMEM((8, 16, D), bf),
            pltpu.VMEM((2, 128, D), bf),
            pltpu.VMEM((128, D), jnp.float32),
            pltpu.VMEM((128, D), bf),
            pltpu.VMEM((N, 2, 96, D), bf),
            pltpu.VMEM((N, 2, 32, D), bf),
            pltpu.VMEM((N, 192, 128), bf),
            pltpu.VMEM((N, 192, 128), bf),
            pltpu.VMEM((64, 2048), bf),
            pltpu.VMEM((2048, 64), bf),
            pltpu.VMEM((64, 2048), bf),
            pltpu.VMEM((N, 64, 128), bf),
            pltpu.VMEM((N, 64, 128), bf),
            pltpu.VMEM((8, 16, NCLS), bf),
            pltpu.VMEM((8, 16, NCLS), bf),
            pltpu.VMEM((N, MOST, 16, NCLS), bf),
            pltpu.VMEM((N, MOST, 16, NCLS), bf),
            pltpu.SemaphoreType.REGULAR,
            dma((N,)), dma((N,)), dma((N,)), dma((N,)), dma((N,)), dma((8,)), dma, dma,
            dma((3,)), dma((12,)), dma((N,)), dma((N,)), dma((N,)),
            dma((3,)), dma((12,)), dma((N,)), dma((N,)), dma((N,)),
            dma((N,)), dma((N,)), dma((N,)), dma((N,)), dma((8,)), dma((8,)), dma((N,)), dma((N,)),
        ],
        compiler_params=pltpu.CompilerParams(
            collective_id=0, has_side_effects=True, vmem_limit_bytes=56 * 1024 * 1024
        ),
    )(
        tile_list, scene_band, pos, wq, wo, norm_gains,
        embed_weight, window_qkv, window_out, head_weight,
    )


def solution(mesh):
    return jax.shard_map(
        local,
        mesh=mesh,
        in_specs=(
            P("seq", "tile", None), P(), P(), P("seq", None), P(), P(), P(),
            P(None, "seq"), P("seq", None), P(),
        ),
        out_specs=P("seq", "tile", None),
        check_vma=False,
    )
```

```python
import functools
import jax
import jax.numpy as jnp
from jax import lax
from jax.experimental import pallas as pl
from jax.experimental.pallas import tpu as pltpu
from jax.sharding import PartitionSpec as P

D = 1024
HD = 64
PADMAX = 16
MOST = 3
N = 16
SC = 96
PV = 768
FH = 384
NCLS = 128
EPSILON = 1e-06
FAR = 4096
NT = (((1,), (1,)), ((), ()))


def layer_norm(stream, gain):
    centre = stream - jnp.mean(stream, axis=-1, keepdims=True)
    spread = jnp.mean(centre * centre, axis=-1, keepdims=True)
    return (centre * lax.rsqrt(spread + EPSILON) * gain).astype(jnp.bfloat16)


def dot(a, b):
    return jnp.dot(a, b, preferred_element_type=jnp.float32)


def remote(src, dst, send_sem, recv_sem, tile, seq):
    return pltpu.make_async_remote_copy(
        src_ref=src, dst_ref=dst, send_sem=send_sem, recv_sem=recv_sem,
        device_id=(tile, seq), device_id_type=pl.DeviceIdType.MESH,
    )


def loop(low, high, body):
    def step(k, carry):
        body(k)
        return carry

    lax.fori_loop(low, high, step, 0)


def kernel(
    tl_hbm, strip, pos, wq, wo, gains, we_hbm, w1_hbm, wout_hbm, hw_hbm, out_ref,
    tl, we, w1, wout, hw, load_sem,
    out1, in1, fwd, pix, posall, nbuf, x_ref, o1,
    wqall, woall, q_out, q_in, qt, kb, vt, o_out, o_in,
    lout, lin, rout, rin,
    entered,
    p1s, p1r, p2s, p2r, pos_s, pos_r, sib_s, sib_r,
    qzs, qxs, qss, qr, qsr, ozs, oxs, oss, orr, osr,
    as_, ar, bs, br, l1s, l1r, l2s, l2r,
):
    i = lax.axis_index("tile")
    r = lax.axis_index("seq")
    core = i % 2
    sibling = i + 1 - 2 * core
    x_at = r // 4
    z_at = r % 4
    band = i // 4
    upper = (i % 4) // 2
    kc_mine = 2 * band + core
    r8 = r // 8
    rm = r % 8

    loads = [
        pltpu.make_async_copy(we_hbm, we, load_sem.at[0]),
        pltpu.make_async_copy(w1_hbm, w1, load_sem.at[1]),
        pltpu.make_async_copy(wout_hbm, wout, load_sem.at[2]),
        pltpu.make_async_copy(hw_hbm, hw, load_sem.at[3]),
        pltpu.make_async_copy(tl_hbm, tl, load_sem.at[4]),
    ]
    for load in loads:
        load.start()

    barrier = pltpu.get_barrier_semaphore()

    def greet(k):
        pl.semaphore_signal(
            barrier, inc=1, device_id=((i + k) % N, r), device_id_type=pl.DeviceIdType.MESH
        )
        pl.semaphore_signal(
            barrier, inc=1, device_id=(i, (r + k) % N), device_id_type=pl.DeviceIdType.MESH
        )

    loop(1, N, greet)

    loads[4].wait()
    owners = [tl[t, 0] for t in range(N)]
    starts = [tl[t, 1] - tl[t, 2] for t in range(N)]
    ranks = []
    for t in range(N):
        rank = jnp.int32(0)
        for u in range(t):
            rank = rank + jnp.where(owners[u] == owners[t], 1, 0)
        ranks.append(jnp.minimum(rank, MOST - 1))
    begin = []
    for m in range(MOST):
        value = jnp.int32(FAR)
        for t in range(N):
            value = jnp.where((owners[t] == i) & (ranks[t] == m), starts[t], value)
        begin.append(value)

    cells = strip[...].reshape(2 * SC, PV)
    token = lax.broadcasted_iota(jnp.int32, (128, 2 * SC), 0)
    cell = lax.broadcasted_iota(jnp.int32, (128, 2 * SC), 1)
    t_row = (token // 8) % 2
    t_col = (token // 16) * 8 + token % 8
    c_row = jnp.where(cell >= SC, 1, 0)
    c_col = cell - SC * c_row
    for m in range(MOST):
        chosen = (c_row == t_row) & (c_col == t_col + begin[m])
        block = dot(jnp.where(chosen, 1.0, 0.0).astype(jnp.bfloat16), cells).astype(jnp.bfloat16)
        for c in range(N):
            k, f = c // 2, c % 2
            out1[c, m] = block[k * 16 : k * 16 + 16, f * FH : f * FH + FH]

    pl.semaphore_wait(barrier, 2 * (N - 1))

    def p1(c):
        return remote(out1.at[c], in1.at[i], p1s.at[c], p1r.at[i], c, r)

    def p1_in(s):
        return remote(out1.at[s], in1.at[s], p1s.at[s], p1r.at[s], s, r)

    loop(1, N, lambda k: p1((i + k) % N).start())
    in1[i] = out1[i]

    def greet_again(k):
        pl.semaphore_signal(
            entered, inc=1, device_id=(i, (r + k) % N), device_id_type=pl.DeviceIdType.MESH
        )

    loop(1, N, greet_again)

    def pos_z(k):
        return remote(
            pos, posall.at[rm], pos_s.at[k - 1], pos_r.at[rm], i, x_at * 4 + (z_at + k) % 4
        )

    block = x_at % 2

    def pos_x(k):
        half = posall.at[pl.ds(4 * block, 4)]
        return remote(
            half, half, pos_s.at[k + 2], pos_r.at[8 + block], i, ((x_at + k) % 4) * 4 + z_at
        )

    def place(dx, dz):
        return ((x_at + dx) % 4) * 4 + (z_at + dz) % 4

    def piece(full, shard, part):
        rows = full.shape[2]
        if part == 2:
            return full.at[shard, core]
        return full.at[shard, core, pl.ds(part * (rows // 2), rows // 2)]

    def along(full, sems, got, step, axis, part, shard, number):
        if axis == 0:
            to = x_at * 4 + (z_at + step) % 4
        else:
            to = ((x_at + step) % 4) * 4 + z_at
        at = piece(full, shard, part)
        return remote(at, at, sems.at[number], got.at[part, shard], i, to)

    def arrived(full, sems, got, part, shard):
        at = piece(full, shard, part)
        remote(at, at, sems.at[0], got.at[part, shard], i, r).wait_recv()

    def to_sibling(full, ss, sgot, shard):
        at = full.at[shard, core]
        return remote(at, at, ss.at[shard], sgot.at[shard], sibling, r)

    def from_sibling(full, ss, sgot, shard):
        at = full.at[shard, 1 - core]
        return remote(at, at, ss.at[shard], sgot.at[shard], sibling, r)

    def gather_copies(full, zs, xs, got):
        result = {}
        for n, step in enumerate((1, 3)):
            result["z", step] = along(full, zs, got, step, 0, 2, place(0, 0), n)
            result["zz", step] = along(full, zs, got, step, 0, n, place(0, 4 - step), 2 + n)
            for dz in range(4):
                result["x", dz, step] = along(
                    full, xs, got, step, 1, 2, place(0, dz), dz * 4 + n
                )
                result["xx", dz, step] = along(
                    full, xs, got, step, 1, n, place(4 - step, dz), dz * 4 + 2 + n
                )
        return result

    def gather_steps(src, full, zs, xs, ss, got, sgot):
        copies = gather_copies(full, zs, xs, got)

        def own():
            full[r] = src[...]
            for step in (1, 3):
                copies["z", step].start()
            for step in (1, 3):
                copies["x", 0, step].start()

        def pass_z():
            for step in (1, 3):
                dz = 4 - step
                arrived(full, zs, got, 2, place(0, dz))
                copies["zz", step].start()
                copies["x", dz, 1].start()
                copies["x", dz, 3].start()
                to_sibling(full, ss, sgot, place(0, dz)).start()

        def pass_zz():
            for part in range(2):
                arrived(full, zs, got, part, place(0, 2))
            copies["x", 2, 1].start()
            copies["x", 2, 3].start()
            to_sibling(full, ss, sgot, place(0, 2)).start()

        def pass_x(dz):
            for step in (1, 3):
                dx = 4 - step
                arrived(full, zs, got, 2, place(dx, dz))
                copies["xx", dz, step].start()
                to_sibling(full, ss, sgot, place(dx, dz)).start()

        def pass_xx(dz):
            for part in range(2):
                arrived(full, zs, got, part, place(2, dz))
            to_sibling(full, ss, sgot, place(2, dz)).start()

        def last():
            loop(1, N, lambda k: from_sibling(full, ss, sgot, (r + k) % N).wait_recv())

        def sent():
            for copy in copies.values():
                copy.wait_send()
            loop(1, N, lambda k: to_sibling(full, ss, sgot, (r + k) % N).wait_send())

        return own, pass_z, pass_zz, pass_x, pass_xx, last, sent

    qg = gather_steps(wq, wqall, qzs, qxs, qss, qr, qsr)
    og = gather_steps(wo, woall, ozs, oxs, oss, orr, osr)

    qg[0]()

    @pl.when(upper == r8)
    def _():
        posall[rm] = pos[...]
        for k in range(1, 4):
            pos_z(k).start()


    loop(1, N, lambda k: p1_in((i + k) % N).wait_recv())
    for t in range(N):
        fwd[t] = in1[owners[t], ranks[t]]
    pl.semaphore_wait(entered, N - 1)

    half_c = (i % 4) // 2
    worker = band * 4 + r8 * 2 + half_c

    def p2(t):
        return remote(
            fwd.at[t], pix.at[core, rm], p2s.at[t], p2r.at[core * 8 + rm], worker, t
        )

    loop(1, N, lambda k: p2((r + k) % N).start())

    @pl.when(worker != i)
    def _():
        p2(r).start()

    @pl.when(worker == i)
    def _():
        pix[core, rm] = fwd[r]

    @pl.when(upper == r8)
    def _():
        for k in range(1, 4):
            other = 4 * block + (z_at + k) % 4
            remote(pos, posall.at[other], pos_s.at[0], pos_r.at[other], i, r).wait_recv()
        for k in range(1, 4):
            pos_x(k).start()

    qg[1]()
    qg[3](0)

    for f in range(2):
        source = band * 4 + core * 2 + f

        def p2_in(k, f=f, source=source):
            @pl.when((source != i) | (upper * 8 + k != r))
            def _():
                remote(
                    fwd.at[0], pix.at[f, k], p2s.at[0], p2r.at[f * 8 + k], i, r
                ).wait_recv()

        loop(0, 8, p2_in)

    for e in range(2):

        @pl.when(2 * upper + e != x_at)
        def _(e=e):
            half = posall.at[pl.ds(4 * e, 4)]
            remote(half, half, pos_s.at[0], pos_r.at[8 + e], i, r).wait_recv()

    loads[0].wait()
    stream = dot(pix[0].reshape(128, FH), we[0:FH]) + dot(pix[1].reshape(128, FH), we[FH:PV])
    stream = stream + posall[...].reshape(128, D).astype(jnp.float32)
    x_ref[...] = stream
    nbuf[core] = layer_norm(stream, gains[0:1])
    sib = remote(nbuf.at[core], nbuf.at[core], sib_s, sib_r, sibling, r)
    sib.start()
    sib_in = remote(nbuf.at[1 - core], nbuf.at[1 - core], sib_s, sib_r, sibling, r)
    qg[2]()
    qg[4](0)
    loads[1].wait()
    sib_in.wait_recv()

    def window_heads(pair):
        columns = w1[:, pl.ds(pl.multiple_of(pair * 384, 384), 384)]
        mine = dot(nbuf[core], columns).astype(jnp.bfloat16)
        other = dot(nbuf[1 - core], columns).astype(jnp.bfloat16)
        both = jnp.concatenate([mine, other], axis=0)
        results = []
        for h in range(2):
            at = h * 192
            scores = lax.dot_general(
                mine[:, at : at + 64], both[:, at + 64 : at + 128], NT,
                preferred_element_type=jnp.float32,
            ) * HD ** (-0.5)
            top = jnp.max(scores, axis=-1, keepdims=True)
            weights = jnp.exp(scores - top)
            weights = weights / jnp.sum(weights, axis=-1, keepdims=True)
            results.append(dot(weights.astype(jnp.bfloat16), both[:, at + 128 : at + 192]))
        o1[:, pl.ds(pl.multiple_of(pair * 128, 128), 128)] = jnp.concatenate(
            results, axis=1
        ).astype(jnp.bfloat16)

    loop(0, 2, window_heads)
    qg[3](1)
    loop(2, 4, window_heads)
    qg[3](3)
    qg[4](1)
    loop(4, 8, window_heads)
    loads[2].wait()
    stream = x_ref[...] + dot(o1[...], wout[...])
    x_ref[...] = stream
    normed = layer_norm(stream, gains[1:2])
    my_head = band * 4 + (i % 4 + 4 - band) % 4

    def to_head(x, z):
        h = x * 4 + z
        return remote(q_out.at[h], q_in.at[i], as_.at[h], ar.at[i], x * 4 + (z + x) % 4, r)

    def project(dz):
        for dx in range(4):
            if dx > 0 or dz > 0:
                from_sibling(wqall, qss, qsr, place(dx, dz)).wait_recv()
        z = (z_at + dz) % 4
        for k in range(4):
            x = (band + k) % 4
            h = x * 4 + z
            q_out[h] = lax.dot_general(
                wqall[h].reshape(192, D), normed, NT, preferred_element_type=jnp.float32
            ).astype(jnp.bfloat16)
            if k > 0:
                to_head(x, z).start()
            else:

                @pl.when(h != my_head)
                def _(x=x, z=z):
                    to_head(x, z).start()

                @pl.when(h == my_head)
                def _(h=h):
                    q_in[i] = q_out[h]

    qg[3](2)
    project(0)
    project(1)
    qg[4](3)
    project(3)
    og[0]()
    qg[4](2)
    project(2)

    def head_in(k):
        s = (i + k) % N
        remote(q_out.at[s], q_in.at[s], as_.at[s], ar.at[s], s, r).wait_recv()

    loop(1, N, head_in)
    for s in range(N):
        at = s * 128
        qt[:, at : at + 128] = q_in[s, 0:64]
        kb[at : at + 128, :] = q_in[s, 64:128].astype(jnp.float32).T.astype(jnp.bfloat16)
        vt[:, at : at + 128] = q_in[s, 128:192]

    def home(j):
        return remote(o_out.at[j], o_in.at[my_head], bs.at[j], br.at[my_head], j, r)

    def attend(k):
        b = (k + i // 2 + 1) % 8
        queries = qt[:, pl.ds(pl.multiple_of(b * 256, 256), 256)]
        scores = dot(kb[...], queries)
        top = jnp.max(scores, axis=0, keepdims=True)
        weights = jnp.exp2((scores - top) * (HD ** (-0.5) * 1.4426950408889634))
        total = jnp.sum(weights, axis=0, keepdims=True)
        mixed = (dot(vt[...], weights.astype(jnp.bfloat16)) / total).astype(jnp.bfloat16)
        o_out[2 * b] = mixed[:, 0:128]
        o_out[2 * b + 1] = mixed[:, 128:256]
        for e in range(2):
            j = 2 * b + e

            @pl.when(j != i)
            def _(j=j):
                home(j).start()

    og[1]()
    og[3](0)
    loop(0, 2, attend)
    og[2]()
    og[4](0)
    og[3](1)
    loop(2, 4, attend)
    og[3](3)
    og[4](1)
    loop(4, 6, attend)
    og[3](2)
    og[4](3)
    loop(6, 8, attend)
    og[4](2)
    o_in[my_head] = o_out[i]
    og[5]()

    def home_in(k):
        s = (my_head + k) % N
        remote(o_out.at[s], o_in.at[s], bs.at[s], br.at[s], i, r).wait_recv()

    loop(1, N, home_in)
    attended = o_in[...].reshape(D, 128).astype(jnp.float32).T.astype(jnp.bfloat16)
    stream = x_ref[...] + dot(attended, woall[...].reshape(D, D))
    loads[3].wait()
    logits = dot(layer_norm(stream, gains[2:3]), hw[...])
    lout[...] = logits.astype(jnp.bfloat16).reshape(8, 16, NCLS)

    collector = 2 * kc_mine + r % 2

    def l1(k):
        return remote(
            lout.at[k], lin.at[r // 2], l1s.at[k], l1r.at[r // 2], collector, upper * 8 + k
        )

    def l1_start(k):
        away = (collector != i) | (upper * 8 + k != r)

        @pl.when(away)
        def _():
            l1(k).start()

        @pl.when(jnp.logical_not(away))
        def _():
            lin[r // 2] = lout[k]

    loop(0, 8, l1_start)
    kc = i // 2
    giver = (kc // 2) * 4 + r8 * 2 + kc % 2

    def l1_in(k):
        @pl.when((giver != i) | (2 * k + i % 2 != r))
        def _():
            remote(lout.at[0], lin.at[k], l1s.at[0], l1r.at[k], i, r).wait_recv()

    slot = [owners[t] * MOST + ranks[t] for t in range(N)]
    lane = lax.broadcasted_iota(jnp.int32, (N * MOST * 16, 128), 1)
    line = lax.broadcasted_iota(jnp.int32, (N * MOST * 16, 128), 0)
    wanted = jnp.zeros((N * MOST * 16, 128), jnp.int32)
    for k in range(8):
        wanted = jnp.where(
            lane // 16 == k, jnp.where(core == 0, slot[2 * k], slot[2 * k + 1]), wanted
        )
    route = jnp.where(line == wanted * 16 + lane % 16, 1.0, 0.0).astype(jnp.bfloat16)
    loop(0, 8, l1_in)
    rout[...] = (
        dot(route, lin[...].reshape(128, NCLS)).astype(jnp.bfloat16).reshape(N, MOST, 16, NCLS)
    )

    def l2(s):
        return remote(rout.at[s], rin.at[i], l2s.at[s], l2r.at[i], s, r)

    loop(1, N, lambda k: l2((i + k) % N).start())
    rin[i] = rout[i]

    cell = lax.broadcasted_iota(jnp.int32, (2 * SC, 128), 0)
    token = lax.broadcasted_iota(jnp.int32, (2 * SC, 128), 1)
    t_row = (token // 8) % 2
    t_col = (token // 16) * 8 + token % 8
    c_row = jnp.where(cell >= SC, 1, 0)
    c_col = cell - SC * c_row
    count = jnp.zeros((2 * SC, 128), jnp.float32)
    spots = []
    for m in range(MOST):
        chosen = (c_row == t_row) & (c_col == t_col + begin[m])
        spots.append(jnp.where(chosen, 1.0, 0.0).astype(jnp.bfloat16))
        count = count + jnp.where((c_col >= begin[m]) & (c_col < begin[m] + 64), 1.0, 0.0)

    def l2_in(k):
        s = (i + k) % N
        remote(rout.at[s], rin.at[s], l2s.at[s], l2r.at[s], s, r).wait_recv()

    loop(1, N, l2_in)
    total = jnp.zeros((2 * SC, NCLS), jnp.float32)
    for m in range(MOST):
        pieces = [rin[2 * k, m] + rin[2 * k + 1, m] for k in range(8)]
        total = total + dot(spots[m], jnp.concatenate(pieces, axis=0))
    out_ref[...] = (total / jnp.maximum(count, 1.0)).reshape(2, SC, NCLS)

    loop(1, N, lambda k: p1((i + k) % N).wait_send())

    @pl.when(upper == r8)
    def _():
        for k in range(1, 4):
            pos_z(k).wait_send()
            pos_x(k).wait_send()

    loop(1, N, lambda k: p2((r + k) % N).wait_send())

    @pl.when(worker != i)
    def _():
        p2(r).wait_send()

    sib.wait_send()
    qg[6]()
    og[6]()
    loop(
        1, N,
        lambda k: to_head(((my_head + k) % N) // 4, (my_head + k) % 4).wait_send(),
    )
    loop(1, N, lambda k: home((i + k) % N).wait_send())

    def l1_sent(k):
        @pl.when((collector != i) | (upper * 8 + k != r))
        def _():
            l1(k).wait_send()

    loop(0, 8, l1_sent)
    loop(1, N, lambda k: l2((i + k) % N).wait_send())


def local(
    scene_band, tile_list, embed_weight, position, norm_gains, window_qkv, window_out,
    global_qkv, global_out, head_weight,
):
    i = lax.axis_index("tile")
    column = 2 * (i // 4) + i % 2
    pos = lax.dynamic_slice_in_dim(position.reshape(2, 64, D), column * 8, 8, 1).reshape(16, D)
    wq = global_qkv.T.reshape(2, 96, D)
    wo = global_out.reshape(2, 32, D)
    bf = jnp.bfloat16
    vmem = pl.BlockSpec(memory_space=pltpu.VMEM)
    hbm = pl.BlockSpec(memory_space=pl.ANY)
    dma = pltpu.SemaphoreType.DMA
    return pl.pallas_call(
        kernel,
        out_shape=jax.ShapeDtypeStruct((2, SC, NCLS), jnp.float32),
        in_specs=[hbm] + [vmem] * 5 + [hbm] * 4,
        out_specs=vmem,
        scratch_shapes=[
            pltpu.SMEM((N, 3), jnp.int32),
            pltpu.VMEM((PV, D), bf),
            pltpu.VMEM((D, 3 * D), bf),
            pltpu.VMEM((D, D), bf),
            pltpu.VMEM((D, NCLS), bf),
            dma((5,)),
            pltpu.VMEM((N, MOST, 16, FH), bf),
            pltpu.VMEM((N, MOST, 16, FH), bf),
            pltpu.VMEM((N, 16, FH), bf),
            pltpu.VMEM((2, 8, 16, FH), bf),
            pltpu.VMEM((8, 16, D), bf),
            pltpu.VMEM((2, 128, D), bf),
            pltpu.VMEM((128, D), jnp.float32),
            pltpu.VMEM((128, D), bf),
            pltpu.VMEM((N, 2, 96, D), bf),
            pltpu.VMEM((N, 2, 32, D), bf),
            pltpu.VMEM((N, 192, 128), bf),
            pltpu.VMEM((N, 192, 128), bf),
            pltpu.VMEM((64, 2048), bf),
            pltpu.VMEM((2048, 64), bf),
            pltpu.VMEM((64, 2048), bf),
            pltpu.VMEM((N, 64, 128), bf),
            pltpu.VMEM((N, 64, 128), bf),
            pltpu.VMEM((8, 16, NCLS), bf),
            pltpu.VMEM((8, 16, NCLS), bf),
            pltpu.VMEM((N, MOST, 16, NCLS), bf),
            pltpu.VMEM((N, MOST, 16, NCLS), bf),
            pltpu.SemaphoreType.REGULAR,
            dma((N,)), dma((N,)), dma((N,)), dma((N,)), dma((6,)), dma((10,)), dma, dma,
            dma((4,)), dma((N,)), dma((N,)), dma((3, N)), dma((N,)),
            dma((4,)), dma((N,)), dma((N,)), dma((3, N)), dma((N,)),
            dma((N,)), dma((N,)), dma((N,)), dma((N,)), dma((8,)), dma((8,)), dma((N,)), dma((N,)),
        ],
        compiler_params=pltpu.CompilerParams(
            collective_id=0, has_side_effects=True, vmem_limit_bytes=56 * 1024 * 1024
        ),
    )(
        tile_list, scene_band, pos, wq, wo, norm_gains,
        embed_weight, window_qkv, window_out, head_weight,
    )


def solution(mesh):
    return jax.shard_map(
        local,
        mesh=mesh,
        in_specs=(
            P("seq", "tile", None), P(), P(), P("seq", None), P(), P(), P(),
            P(None, "seq"), P("seq", None), P(),
        ),
        out_specs=P("seq", "tile", None),
        check_vma=False,
    )
```

```python
import functools
import jax
import jax.numpy as jnp
from jax import lax
from jax.experimental import pallas as pl
from jax.experimental.pallas import tpu as pltpu
from jax.sharding import PartitionSpec as P

D = 1024
HD = 64
PADMAX = 16
MOST = 3
N = 16
SC = 96
PV = 768
FH = 384
NCLS = 128
EPSILON = 1e-06
FAR = 4096
NT = (((1,), (1,)), ((), ()))


def layer_norm(stream, gain):
    centre = stream - jnp.mean(stream, axis=-1, keepdims=True)
    spread = jnp.mean(centre * centre, axis=-1, keepdims=True)
    return (centre * lax.rsqrt(spread + EPSILON) * gain).astype(jnp.bfloat16)


def dot(a, b):
    return jnp.dot(a, b, preferred_element_type=jnp.float32)


def remote(src, dst, send_sem, recv_sem, tile, seq):
    return pltpu.make_async_remote_copy(
        src_ref=src, dst_ref=dst, send_sem=send_sem, recv_sem=recv_sem,
        device_id=(tile, seq), device_id_type=pl.DeviceIdType.MESH,
    )


def loop(low, high, body):
    def step(k, carry):
        body(k)
        return carry

    lax.fori_loop(low, high, step, 0)


def kernel(
    tl_hbm, strip, pos, wq, wo, gains, we_hbm, w1_hbm, wout_hbm, hw_hbm, out_ref,
    tl, we, w1, wout, hw, load_sem,
    out1, in1, fwd, pix, posall, nbuf, x_ref, o1,
    wqall, woall, q_out, q_in, qt, kb, vt, o_out, o_in,
    lout, lin, rout, rin,
    nall, entered, ns, nr,
    p1s, p1r, p2s, p2r, pos_s, pos_r, sib_s, sib_r,
    qzs, qss, qr, qsr, ozs, oxs, oss, orr, osr,
    as_, ar, bs, br, l1s, l1r, l2s, l2r,
):
    i = lax.axis_index("tile")
    r = lax.axis_index("seq")
    core = i % 2
    sibling = i + 1 - 2 * core
    x_at = r // 4
    z_at = r % 4
    y_at = i // 4
    z_low = (i % 4) // 2
    y_high = y_at // 2
    upper = y_at % 2
    kc_mine = 2 * x_at + core
    my_tile = z_at * 4 + z_low * 2 + y_high
    fourth = upper * 2 + core
    my_head = x_at * 4 + fourth
    r8 = r // 8
    rm = r % 8

    def worker(t, a, b, half):
        return ((t % 2) * 2 + a) * 4 + ((t // 2) % 2) * 2 + half, b * 4 + t // 4

    def member(quarter):
        return (y_high * 2 + quarter // 2) * 4 + z_low * 2 + quarter % 2

    loads = [
        pltpu.make_async_copy(we_hbm, we, load_sem.at[0]),
        pltpu.make_async_copy(w1_hbm, w1, load_sem.at[1]),
        pltpu.make_async_copy(wout_hbm, wout, load_sem.at[2]),
        pltpu.make_async_copy(hw_hbm, hw, load_sem.at[3]),
        pltpu.make_async_copy(tl_hbm, tl, load_sem.at[4]),
    ]
    for load in loads:
        load.start()

    barrier = pltpu.get_barrier_semaphore()

    def greet(k):
        pl.semaphore_signal(
            barrier, inc=1, device_id=((i + k) % N, r), device_id_type=pl.DeviceIdType.MESH
        )
        pl.semaphore_signal(
            barrier, inc=1, device_id=(i, (r + k) % N), device_id_type=pl.DeviceIdType.MESH
        )

    loop(1, N, greet)

    loads[4].wait()
    owners = [tl[t, 0] for t in range(N)]
    starts = [tl[t, 1] - tl[t, 2] for t in range(N)]
    ranks = []
    for t in range(N):
        rank = jnp.int32(0)
        for u in range(t):
            rank = rank + jnp.where(owners[u] == owners[t], 1, 0)
        ranks.append(jnp.minimum(rank, MOST - 1))
    begin = []
    for m in range(MOST):
        value = jnp.int32(FAR)
        for t in range(N):
            value = jnp.where((owners[t] == i) & (ranks[t] == m), starts[t], value)
        begin.append(value)

    cells = strip[...].reshape(2 * SC, PV)
    token = lax.broadcasted_iota(jnp.int32, (128, 2 * SC), 0)
    cell = lax.broadcasted_iota(jnp.int32, (128, 2 * SC), 1)
    t_row = (token // 8) % 2
    t_col = (token // 16) * 8 + token % 8
    c_row = jnp.where(cell >= SC, 1, 0)
    c_col = cell - SC * c_row
    for m in range(MOST):
        chosen = (c_row == t_row) & (c_col == t_col + begin[m])
        block = dot(jnp.where(chosen, 1.0, 0.0).astype(jnp.bfloat16), cells).astype(jnp.bfloat16)
        for c in range(N):
            k, f = c // 2, c % 2
            out1[c, m] = block[k * 16 : k * 16 + 16, f * FH : f * FH + FH]

    pl.semaphore_wait(barrier, 2 * (N - 1))

    def p1(c):
        return remote(out1.at[c], in1.at[i], p1s.at[c], p1r.at[i], c, r)

    def p1_in(s):
        return remote(out1.at[s], in1.at[s], p1s.at[s], p1r.at[s], s, r)

    loop(1, N, lambda k: p1((i + k) % N).start())
    in1[i] = out1[i]

    def greet_again(k):
        pl.semaphore_signal(
            entered, inc=1, device_id=(i, (r + k) % N), device_id_type=pl.DeviceIdType.MESH
        )

    loop(1, N, greet_again)

    aside = jnp.where(upper == r8, 0, 1)

    def pos_copy(n):
        to = 2 * (n // 4) + aside
        return remote(
            pos.at[to], posall.at[rm], pos_s.at[n], pos_r.at[rm],
            i + aside * (4 - 8 * upper), to * 4 + n % 4,
        )

    def pos_stays(n):
        return (aside == 0) & ((2 * (n // 4)) * 4 + n % 4 == r)

    def pos_start(n):
        @pl.when(jnp.logical_not(pos_stays(n)))
        def _():
            pos_copy(n).start()

        @pl.when(pos_stays(n))
        def _():
            posall[rm] = pos[x_at]

    def pos_sent(n):
        @pl.when(jnp.logical_not(pos_stays(n)))
        def _():
            pos_copy(n).wait_send()

    def place(dx, dz):
        return ((x_at + dx) % 4) * 4 + (z_at + dz) % 4

    def piece(full, shard, part):
        rows = full.shape[2]
        if part == 2:
            return full.at[shard, core]
        return full.at[shard, core, pl.ds(part * (rows // 2), rows // 2)]

    def along(full, sems, got, step, axis, part, shard, number):
        if axis == 0:
            to = x_at * 4 + (z_at + step) % 4
        else:
            to = ((x_at + step) % 4) * 4 + z_at
        at = piece(full, shard, part)
        return remote(at, at, sems.at[number], got.at[part, shard], i, to)

    def arrived(full, sems, got, part, shard):
        at = piece(full, shard, part)
        remote(at, at, sems.at[0], got.at[part, shard], i, r).wait_recv()

    def to_sibling(full, ss, sgot, shard):
        at = full.at[shard, core]
        return remote(at, at, ss.at[shard], sgot.at[shard], sibling, r)

    def from_sibling(full, ss, sgot, shard):
        at = full.at[shard, 1 - core]
        return remote(at, at, ss.at[shard], sgot.at[shard], sibling, r)

    def gather_copies(full, zs, xs, got):
        result = {}
        for n, step in enumerate((1, 3)):
            result["z", step] = along(full, zs, got, step, 0, 2, place(0, 0), n)
            result["zz", step] = along(full, zs, got, step, 0, n, place(0, 4 - step), 2 + n)
            for dz in range(4):
                result["x", dz, step] = along(
                    full, xs, got, step, 1, 2, place(0, dz), dz * 4 + n
                )
                result["xx", dz, step] = along(
                    full, xs, got, step, 1, n, place(4 - step, dz), dz * 4 + 2 + n
                )
        return result

    def gather_steps(src, full, zs, xs, ss, got, sgot):
        copies = gather_copies(full, zs, xs, got)

        def own():
            full[r] = src[...]
            for step in (1, 3):
                copies["z", step].start()
            for step in (1, 3):
                copies["x", 0, step].start()

        def pass_z():
            for step in (1, 3):
                dz = 4 - step
                arrived(full, zs, got, 2, place(0, dz))
                copies["zz", step].start()
                copies["x", dz, 1].start()
                copies["x", dz, 3].start()
                to_sibling(full, ss, sgot, place(0, dz)).start()

        def pass_zz():
            for part in range(2):
                arrived(full, zs, got, part, place(0, 2))
            copies["x", 2, 1].start()
            copies["x", 2, 3].start()
            to_sibling(full, ss, sgot, place(0, 2)).start()

        def pass_x(dz):
            for step in (1, 3):
                dx = 4 - step
                arrived(full, zs, got, 2, place(dx, dz))
                copies["xx", dz, step].start()
                to_sibling(full, ss, sgot, place(dx, dz)).start()

        def pass_xx(dz):
            for part in range(2):
                arrived(full, zs, got, part, place(2, dz))
            to_sibling(full, ss, sgot, place(2, dz)).start()

        def last():
            loop(1, N, lambda k: from_sibling(full, ss, sgot, (r + k) % N).wait_recv())

        def sent():
            for copy in copies.values():
                copy.wait_send()
            loop(1, N, lambda k: to_sibling(full, ss, sgot, (r + k) % N).wait_send())

        return own, pass_z, pass_zz, pass_x, pass_xx, last, sent

    def weights_at(z, part):
        if part == 2:
            return wqall.at[z % 4, core]
        return wqall.at[z % 4, core, pl.ds(part * 48, 48)]

    def weights_z(step, part, z, number):
        at = weights_at(z, part)
        return remote(
            at, at, qzs.at[number], qr.at[part, z % 4], i, x_at * 4 + (z_at + step) % 4
        )

    weights_copies = [
        weights_z(1, 2, z_at, 0),
        weights_z(3, 2, z_at, 1),
        weights_z(1, 0, z_at + 3, 2),
        weights_z(3, 1, z_at + 1, 3),
    ]

    def weights_in(z, part):
        at = weights_at(z, part)
        remote(at, at, qzs.at[0], qr.at[part, z % 4], i, r).wait_recv()

    def weights_sibling(k):
        z = (z_at + k) % 4
        at = wqall.at[z, core]
        return remote(at, at, qss.at[z], qsr.at[z], sibling, r)

    def pass_weights():
        weights_in(z_at + 3, 2)
        weights_copies[2].start()
        weights_sibling(3).start()
        weights_in(z_at + 1, 2)
        weights_copies[3].start()
        weights_sibling(1).start()

    def pass_weights_last():
        weights_in(z_at + 2, 0)
        weights_in(z_at + 2, 1)
        weights_sibling(2).start()

    og = gather_steps(wo, woall, ozs, oxs, oss, orr, osr)

    pl.semaphore_wait(entered, N - 1)
    loop(0, 8, pos_start)
    loop(1, N, lambda k: p1_in((i + k) % N).wait_recv())
    for t in range(N):
        fwd[t] = in1[owners[t], ranks[t]]

    def p2(t):
        tile, seq = worker(t, r8, y_at, z_low)
        return remote(
            fwd.at[t], pix.at[core, rm], p2s.at[t], p2r.at[core * 8 + rm], tile, seq
        )

    home_tile, home_seq = worker(my_tile, r8, y_at, z_low)
    away = (home_tile != i) | (home_seq != r)
    loop(1, N, lambda k: p2((my_tile + k) % N).start())

    @pl.when(away)
    def _():
        p2(my_tile).start()

    @pl.when(jnp.logical_not(away))
    def _():
        pix[core, rm] = fwd[my_tile]

    for f in range(2):
        source = 2 * kc_mine + f

        def p2_in(k, f=f, source=source):
            @pl.when((source != i) | (upper * 8 + k != r))
            def _():
                remote(
                    fwd.at[0], pix.at[f, k], p2s.at[0], p2r.at[f * 8 + k], i, r
                ).wait_recv()

        loop(0, 8, p2_in)

    def pos_in(k):
        @pl.when((upper * 8 + k != r) | (x_at % 2 == 1))
        def _():
            remote(pos.at[0], posall.at[k], pos_s.at[0], pos_r.at[k], i, r).wait_recv()

    loop(0, 8, pos_in)
    wqall[z_at] = wq[...]
    og[0]()
    weights_copies[0].start()
    weights_copies[1].start()
    loads[0].wait()
    stream = dot(pix[0].reshape(128, FH), we[0:FH]) + dot(pix[1].reshape(128, FH), we[FH:PV])
    stream = stream + posall[...].reshape(128, D).astype(jnp.float32)
    x_ref[...] = stream
    nbuf[core] = layer_norm(stream, gains[0:1])
    sib = remote(nbuf.at[core], nbuf.at[core], sib_s, sib_r, sibling, r)
    sib.start()
    sib_in = remote(nbuf.at[1 - core], nbuf.at[1 - core], sib_s, sib_r, sibling, r)
    og[1]()
    og[3](0)
    loads[1].wait()
    sib_in.wait_recv()

    def window_heads(pair):
        columns = w1[:, pl.ds(pl.multiple_of(pair * 384, 384), 384)]
        mine = dot(nbuf[core], columns).astype(jnp.bfloat16)
        other = dot(nbuf[1 - core], columns).astype(jnp.bfloat16)
        both = jnp.concatenate([mine, other], axis=0)
        results = []
        for h in range(2):
            at = h * 192
            scores = lax.dot_general(
                mine[:, at : at + 64], both[:, at + 64 : at + 128], NT,
                preferred_element_type=jnp.float32,
            ) * HD ** (-0.5)
            top = jnp.max(scores, axis=-1, keepdims=True)
            weights = jnp.exp(scores - top)
            weights = weights / jnp.sum(weights, axis=-1, keepdims=True)
            results.append(dot(weights.astype(jnp.bfloat16), both[:, at + 128 : at + 192]))
        o1[:, pl.ds(pl.multiple_of(pair * 128, 128), 128)] = jnp.concatenate(
            results, axis=1
        ).astype(jnp.bfloat16)

    loop(0, 2, window_heads)
    og[2]()
    pass_weights()
    loop(2, 4, window_heads)
    og[4](0)
    og[3](1)
    loop(4, 6, window_heads)
    og[3](3)
    og[4](1)
    loop(6, 8, window_heads)
    og[3](2)
    og[4](3)
    pass_weights_last()
    loads[2].wait()
    stream = x_ref[...] + dot(o1[...], wout[...])
    x_ref[...] = stream
    nall[x_at] = layer_norm(stream, gains[1:2])

    def tokens_x(k):
        at = nall.at[x_at]
        return remote(at, at, ns.at[k - 1], nr.at[x_at], i, ((x_at + k) % 4) * 4 + z_at)

    for k in (1, 3, 2):
        tokens_x(k).start()
    for k in range(1, 4):
        z = (z_at + k) % 4
        at = wqall.at[z, 1 - core]
        remote(at, at, qss.at[z], qsr.at[z], sibling, r).wait_recv()

    def to_head(x, k):
        quarter = (fourth + k) % 4
        at = q_out.at[x * 4 + quarter]
        return remote(
            at, q_in.at[x * 4 + fourth], as_.at[x * 4 + quarter], ar.at[x * 4 + fourth],
            member(quarter), r,
        )

    for step in (0, 1, 3, 2):
        x = (x_at + step) % 4
        if step > 0:
            at = nall.at[x]
            remote(at, at, ns.at[0], nr.at[x], i, r).wait_recv()
        tokens = nall[x]
        for k in (1, 2, 3, 0):
            quarter = (fourth + k) % 4
            found = lax.dot_general(
                wqall[quarter].reshape(192, D), tokens, NT, preferred_element_type=jnp.float32
            ).astype(jnp.bfloat16)
            if k > 0:
                q_out[x * 4 + quarter] = found
                to_head(x, k).start()
            else:
                q_in[x * 4 + fourth] = found

    def head_in(x):
        for k in range(1, 4):
            s = x * 4 + (fourth + k) % 4
            remote(q_out.at[s], q_in.at[s], as_.at[s], ar.at[s], i, r).wait_recv()

    loop(0, 4, head_in)
    for s in range(N):
        at = s * 128
        qt[:, at : at + 128] = q_in[s, 0:64]
        kb[at : at + 128, :] = q_in[s, 64:128].astype(jnp.float32).T.astype(jnp.bfloat16)
        vt[:, at : at + 128] = q_in[s, 128:192]

    def home(j):
        return remote(
            o_out.at[j], o_in.at[my_head], bs.at[j], br.at[my_head],
            member(j % 4), (j // 4) * 4 + z_at,
        )

    def attend(k):
        b = (k + my_head // 2 + 1) % 8
        queries = qt[:, pl.ds(pl.multiple_of(b * 256, 256), 256)]
        scores = dot(kb[...], queries)
        top = jnp.max(scores, axis=0, keepdims=True)
        weights = jnp.exp2((scores - top) * (HD ** (-0.5) * 1.4426950408889634))
        total = jnp.sum(weights, axis=0, keepdims=True)
        mixed = (dot(vt[...], weights.astype(jnp.bfloat16)) / total).astype(jnp.bfloat16)
        o_out[2 * b] = mixed[:, 0:128]
        o_out[2 * b + 1] = mixed[:, 128:256]
        for e in range(2):
            j = 2 * b + e

            @pl.when(j != my_head)
            def _(j=j):
                home(j).start()

    og[4](2)
    loop(0, 8, attend)
    o_in[my_head] = o_out[my_head]
    og[5]()

    def home_in(k):
        s = (my_head + k) % N
        remote(o_out.at[s], o_in.at[s], bs.at[s], br.at[s], i, r).wait_recv()

    loop(1, N, home_in)
    attended = o_in[...].reshape(D, 128).astype(jnp.float32).T.astype(jnp.bfloat16)
    stream = x_ref[...] + dot(attended, woall[...].reshape(D, D))
    loads[3].wait()
    logits = dot(layer_norm(stream, gains[2:3]), hw[...])
    lout[...] = logits.astype(jnp.bfloat16).reshape(8, 16, NCLS)

    collector = 2 * kc_mine + my_tile % 2

    def l1(k):
        return remote(
            lout.at[k], lin.at[my_tile // 2], l1s.at[k], l1r.at[my_tile // 2], collector, upper * 8 + k
        )

    def l1_start(k):
        away = (collector != i) | (upper * 8 + k != r)

        @pl.when(away)
        def _():
            l1(k).start()

        @pl.when(jnp.logical_not(away))
        def _():
            lin[my_tile // 2] = lout[k]

    loop(0, 8, l1_start)
    kc = i // 2

    def l1_in(k):
        giver, at = worker(2 * k + i % 2, r8, kc // 2, kc % 2)

        @pl.when((giver != i) | (at != r))
        def _():
            remote(lout.at[0], lin.at[k], l1s.at[0], l1r.at[k], i, r).wait_recv()

    slot = [owners[t] * MOST + ranks[t] for t in range(N)]
    lane = lax.broadcasted_iota(jnp.int32, (N * MOST * 16, 128), 1)
    line = lax.broadcasted_iota(jnp.int32, (N * MOST * 16, 128), 0)
    wanted = jnp.zeros((N * MOST * 16, 128), jnp.int32)
    for k in range(8):
        wanted = jnp.where(
            lane // 16 == k, jnp.where(core == 0, slot[2 * k], slot[2 * k + 1]), wanted
        )
    route = jnp.where(line == wanted * 16 + lane % 16, 1.0, 0.0).astype(jnp.bfloat16)
    loop(0, 8, l1_in)
    rout[...] = (
        dot(route, lin[...].reshape(128, NCLS)).astype(jnp.bfloat16).reshape(N, MOST, 16, NCLS)
    )

    def l2(s):
        return remote(rout.at[s], rin.at[i], l2s.at[s], l2r.at[i], s, r)

    loop(1, N, lambda k: l2((i + k) % N).start())
    rin[i] = rout[i]

    cell = lax.broadcasted_iota(jnp.int32, (2 * SC, 128), 0)
    token = lax.broadcasted_iota(jnp.int32, (2 * SC, 128), 1)
    t_row = (token // 8) % 2
    t_col = (token // 16) * 8 + token % 8
    c_row = jnp.where(cell >= SC, 1, 0)
    c_col = cell - SC * c_row
    count = jnp.zeros((2 * SC, 128), jnp.float32)
    spots = []
    for m in range(MOST):
        chosen = (c_row == t_row) & (c_col == t_col + begin[m])
        spots.append(jnp.where(chosen, 1.0, 0.0).astype(jnp.bfloat16))
        count = count + jnp.where((c_col >= begin[m]) & (c_col < begin[m] + 64), 1.0, 0.0)

    def l2_in(k):
        s = (i + k) % N
        remote(rout.at[s], rin.at[s], l2s.at[s], l2r.at[s], s, r).wait_recv()

    loop(1, N, l2_in)
    total = jnp.zeros((2 * SC, NCLS), jnp.float32)
    for m in range(MOST):
        pieces = [rin[2 * k, m] + rin[2 * k + 1, m] for k in range(8)]
        total = total + dot(spots[m], jnp.concatenate(pieces, axis=0))
    out_ref[...] = (total / jnp.maximum(count, 1.0)).reshape(2, SC, NCLS)

    loop(1, N, lambda k: p1((i + k) % N).wait_send())

    loop(0, 8, pos_sent)
    loop(1, N, lambda k: p2((my_tile + k) % N).wait_send())

    @pl.when(away)
    def _():
        p2(my_tile).wait_send()

    sib.wait_send()
    for k in range(1, 4):
        weights_sibling(k).wait_send()
        tokens_x(k).wait_send()
    for copy in weights_copies:
        copy.wait_send()
    og[6]()

    def heads_sent(x):
        for k in range(1, 4):
            to_head(x, k).wait_send()

    loop(0, 4, heads_sent)
    loop(1, N, lambda k: home((my_head + k) % N).wait_send())

    def l1_sent(k):
        @pl.when((collector != i) | (upper * 8 + k != r))
        def _():
            l1(k).wait_send()

    loop(0, 8, l1_sent)
    loop(1, N, lambda k: l2((i + k) % N).wait_send())


def local(
    scene_band, tile_list, embed_weight, position, norm_gains, window_qkv, window_out,
    global_qkv, global_out, head_weight,
):
    core = lax.axis_index("tile") % 2
    parts = position.reshape(2, 4, 2, 8, D)
    pos = lax.dynamic_index_in_dim(parts, core, 2, False).transpose(1, 0, 2, 3).reshape(4, 16, D)
    wq = global_qkv.T.reshape(2, 96, D)
    wo = global_out.reshape(2, 32, D)
    bf = jnp.bfloat16
    vmem = pl.BlockSpec(memory_space=pltpu.VMEM)
    hbm = pl.BlockSpec(memory_space=pl.ANY)
    dma = pltpu.SemaphoreType.DMA
    return pl.pallas_call(
        kernel,
        out_shape=jax.ShapeDtypeStruct((2, SC, NCLS), jnp.float32),
        in_specs=[hbm] + [vmem] * 5 + [hbm] * 4,
        out_specs=vmem,
        scratch_shapes=[
            pltpu.SMEM((N, 3), jnp.int32),
            pltpu.VMEM((PV, D), bf),
            pltpu.VMEM((D, 3 * D), bf),
            pltpu.VMEM((D, D), bf),
            pltpu.VMEM((D, NCLS), bf),
            dma((5,)),
            pltpu.VMEM((N, MOST, 16, FH), bf),
            pltpu.VMEM((N, MOST, 16, FH), bf),
            pltpu.VMEM((N, 16, FH), bf),
            pltpu.VMEM((2, 8, 16, FH), bf),
            pltpu.VMEM((8, 16, D), bf),
            pltpu.VMEM((2, 128, D), bf),
            pltpu.VMEM((128, D), jnp.float32),
            pltpu.VMEM((128, D), bf),
            pltpu.VMEM((4, 2, 96, D), bf),
            pltpu.VMEM((N, 2, 32, D), bf),
            pltpu.VMEM((N, 192, 128), bf),
            pltpu.VMEM((N, 192, 128), bf),
            pltpu.VMEM((64, 2048), bf),
            pltpu.VMEM((2048, 64), bf),
            pltpu.VMEM((64, 2048), bf),
            pltpu.VMEM((N, 64, 128), bf),
            pltpu.VMEM((N, 64, 128), bf),
            pltpu.VMEM((8, 16, NCLS), bf),
            pltpu.VMEM((8, 16, NCLS), bf),
            pltpu.VMEM((N, MOST, 16, NCLS), bf),
            pltpu.VMEM((N, MOST, 16, NCLS), bf),
            pltpu.VMEM((4, 128, D), bf),
            pltpu.SemaphoreType.REGULAR,
            dma((3,)), dma((4,)),
            dma((N,)), dma((N,)), dma((N,)), dma((N,)), dma((8,)), dma((8,)), dma, dma,
            dma((4,)), dma((4,)), dma((3, 4)), dma((4,)),
            dma((4,)), dma((N,)), dma((N,)), dma((3, N)), dma((N,)),
            dma((N,)), dma((N,)), dma((N,)), dma((N,)), dma((8,)), dma((8,)), dma((N,)), dma((N,)),
        ],
        compiler_params=pltpu.CompilerParams(
            collective_id=0, has_side_effects=True, vmem_limit_bytes=56 * 1024 * 1024
        ),
    )(
        tile_list, scene_band, pos, wq, wo, norm_gains,
        embed_weight, window_qkv, window_out, head_weight,
    )


def solution(mesh):
    return jax.shard_map(
        local,
        mesh=mesh,
        in_specs=(
            P("seq", "tile", None), P(), P(), P("seq", None), P(), P(), P(),
            P(None, "seq"), P("seq", None), P(),
        ),
        out_specs=P("seq", "tile", None),
        check_vma=False,
    )
```

```python
import functools
import jax
import jax.numpy as jnp
from jax import lax
from jax.experimental import pallas as pl
from jax.experimental.pallas import tpu as pltpu
from jax.sharding import PartitionSpec as P

D = 1024
HD = 64
PADMAX = 16
MOST = 3
N = 16
SC = 96
PV = 768
FH = 384
NCLS = 128
EPSILON = 1e-06
FAR = 4096
NT = (((1,), (1,)), ((), ()))


def layer_norm(stream, gain):
    centre = stream - jnp.mean(stream, axis=-1, keepdims=True)
    spread = jnp.mean(centre * centre, axis=-1, keepdims=True)
    return (centre * lax.rsqrt(spread + EPSILON) * gain).astype(jnp.bfloat16)


def dot(a, b):
    return jnp.dot(a, b, preferred_element_type=jnp.float32)


def remote(src, dst, send_sem, recv_sem, tile, seq):
    return pltpu.make_async_remote_copy(
        src_ref=src, dst_ref=dst, send_sem=send_sem, recv_sem=recv_sem,
        device_id=(tile, seq), device_id_type=pl.DeviceIdType.MESH,
    )


def loop(low, high, body):
    def step(k, carry):
        body(k)
        return carry

    lax.fori_loop(low, high, step, 0)


def kernel(
    tl_hbm, strip, pos, wq, wo, gains, we_hbm, w1_hbm, wout_hbm, hw_hbm, out_ref,
    tl, we, w1, wout, hw, load_sem,
    out1, in1, fwd, pix, posall, nbuf, x_ref, o1,
    wqall, woall, q_out, q_in, qt, kb, vt, o_out, o_in,
    lout, lin, rout, rin,
    nall, entered, ns, nr,
    p1s, p1r, p2s, p2r, pos_s, pos_r, sib_s, sib_r,
    qzs, qss, qr, qsr, ozs, oxs, oss, obs, ozr, oxr, osr, obr,
    as_, ar, bs, br, l1s, l1r, l2s, l2r,
):
    i = lax.axis_index("tile")
    r = lax.axis_index("seq")
    core = i % 2
    sibling = i + 1 - 2 * core
    x_at = r // 4
    z_at = r % 4
    y_at = i // 4
    z_low = (i % 4) // 2
    y_high = y_at // 2
    upper = y_at % 2
    kc_mine = 2 * x_at + core
    my_tile = z_at * 4 + z_low * 2 + y_high
    fourth = upper * 2 + core
    my_head = x_at * 4 + fourth
    r8 = r // 8
    rm = r % 8

    def worker(t, a, b, half):
        return ((t % 2) * 2 + a) * 4 + ((t // 2) % 2) * 2 + half, b * 4 + t // 4

    def member(quarter):
        return (y_high * 2 + quarter // 2) * 4 + z_low * 2 + quarter % 2

    loads = [
        pltpu.make_async_copy(we_hbm, we, load_sem.at[0]),
        pltpu.make_async_copy(w1_hbm, w1, load_sem.at[1]),
        pltpu.make_async_copy(wout_hbm, wout, load_sem.at[2]),
        pltpu.make_async_copy(hw_hbm, hw, load_sem.at[3]),
        pltpu.make_async_copy(tl_hbm, tl, load_sem.at[4]),
    ]
    for load in loads:
        load.start()

    barrier = pltpu.get_barrier_semaphore()

    def greet(k):
        pl.semaphore_signal(
            barrier, inc=1, device_id=((i + k) % N, r), device_id_type=pl.DeviceIdType.MESH
        )
        pl.semaphore_signal(
            barrier, inc=1, device_id=(i, (r + k) % N), device_id_type=pl.DeviceIdType.MESH
        )

    loop(1, N, greet)

    loads[4].wait()
    owners = [tl[t, 0] for t in range(N)]
    starts = [tl[t, 1] - tl[t, 2] for t in range(N)]
    ranks = []
    for t in range(N):
        rank = jnp.int32(0)
        for u in range(t):
            rank = rank + jnp.where(owners[u] == owners[t], 1, 0)
        ranks.append(jnp.minimum(rank, MOST - 1))
    begin = []
    for m in range(MOST):
        value = jnp.int32(FAR)
        for t in range(N):
            value = jnp.where((owners[t] == i) & (ranks[t] == m), starts[t], value)
        begin.append(value)

    cells = strip[...].reshape(2 * SC, PV)
    token = lax.broadcasted_iota(jnp.int32, (128, 2 * SC), 0)
    cell = lax.broadcasted_iota(jnp.int32, (128, 2 * SC), 1)
    t_row = (token // 8) % 2
    t_col = (token // 16) * 8 + token % 8
    c_row = jnp.where(cell >= SC, 1, 0)
    c_col = cell - SC * c_row
    for m in range(MOST):
        chosen = (c_row == t_row) & (c_col == t_col + begin[m])
        block = dot(jnp.where(chosen, 1.0, 0.0).astype(jnp.bfloat16), cells).astype(jnp.bfloat16)
        for c in range(N):
            k, f = c // 2, c % 2
            out1[c, m] = block[k * 16 : k * 16 + 16, f * FH : f * FH + FH]

    pl.semaphore_wait(barrier, 2 * (N - 1))

    def p1(c):
        return remote(out1.at[c], in1.at[i], p1s.at[c], p1r.at[i], c, r)

    def p1_in(s):
        return remote(out1.at[s], in1.at[s], p1s.at[s], p1r.at[s], s, r)

    loop(1, N, lambda k: p1((i + k) % N).start())
    in1[i] = out1[i]

    def greet_again(k):
        pl.semaphore_signal(
            entered, inc=1, device_id=(i, (r + k) % N), device_id_type=pl.DeviceIdType.MESH
        )

    loop(1, N, greet_again)

    aside = jnp.where(upper == r8, 0, 1)

    def pos_copy(n):
        to = 2 * (n // 4) + aside
        return remote(
            pos.at[to], posall.at[rm], pos_s.at[n], pos_r.at[rm],
            i + aside * (4 - 8 * upper), to * 4 + n % 4,
        )

    def pos_stays(n):
        return (aside == 0) & ((2 * (n // 4)) * 4 + n % 4 == r)

    def pos_start(n):
        @pl.when(jnp.logical_not(pos_stays(n)))
        def _():
            pos_copy(n).start()

        @pl.when(pos_stays(n))
        def _():
            posall[rm] = pos[x_at]

    def pos_sent(n):
        @pl.when(jnp.logical_not(pos_stays(n)))
        def _():
            pos_copy(n).wait_send()

    def place(dx, dz):
        return ((x_at + dx) % 4) * 4 + (z_at + dz) % 4

    def weights_at(z, part):
        if part == 2:
            return wqall.at[z % 4, core]
        return wqall.at[z % 4, core, pl.ds(part * 48, 48)]

    def weights_z(step, part, z, number):
        at = weights_at(z, part)
        return remote(
            at, at, qzs.at[number], qr.at[part, z % 4], i, x_at * 4 + (z_at + step) % 4
        )

    weights_copies = [
        weights_z(1, 2, z_at, 0),
        weights_z(3, 2, z_at, 1),
        weights_z(1, 0, z_at + 3, 2),
        weights_z(3, 1, z_at + 1, 3),
    ]

    def weights_in(z, part):
        at = weights_at(z, part)
        remote(at, at, qzs.at[0], qr.at[part, z % 4], i, r).wait_recv()

    def weights_sibling(k):
        z = (z_at + k) % 4
        at = wqall.at[z, core]
        return remote(at, at, qss.at[z], qsr.at[z], sibling, r)

    def pass_weights():
        weights_in(z_at + 3, 2)
        weights_copies[2].start()
        weights_sibling(3).start()
        weights_in(z_at + 1, 2)
        weights_copies[3].start()
        weights_sibling(1).start()

    def pass_weights_last():
        weights_in(z_at + 2, 0)
        weights_in(z_at + 2, 1)
        weights_sibling(2).start()

    def out_z(k):
        return remote(
            wo.at[core], woall.at[r, core], ozs.at[k - 1], ozr.at[z_at],
            i, x_at * 4 + (z_at + k) % 4,
        )

    def out_z_sibling(k):
        z = (z_at + k) % 4
        at = woall.at[x_at * 4 + z, core]
        return remote(at, at, oss.at[k - 1], osr.at[z], sibling, r)

    def out_x(k):
        at = woall.at[pl.ds(4 * x_at, 4), core]
        return remote(at, at, oxs.at[k - 1], oxr.at[x_at], i, ((x_at + k) % 4) * 4 + z_at)

    def out_x_sibling(k):
        x = (x_at + k) % 4
        at = woall.at[pl.ds(4 * x, 4), core]
        return remote(at, at, obs.at[k - 1], obr.at[x], sibling, r)

    def out_own():
        woall[r] = wo[...]
        for k in range(1, 4):
            out_z(k).start()

    def out_pass_z():
        for k in range(1, 4):
            z = (z_at + k) % 4
            remote(
                wo.at[core], woall.at[x_at * 4 + z, core], ozs.at[0], ozr.at[z], i, r
            ).wait_recv()
        for k in (1, 3, 2):
            out_x(k).start()
        for k in range(1, 4):
            out_z_sibling(k).start()

    def out_pass_x():
        for k in (1, 3, 2):
            x = (x_at + k) % 4
            at = woall.at[pl.ds(4 * x, 4), core]
            remote(at, at, oxs.at[0], oxr.at[x], i, r).wait_recv()
            out_x_sibling(k).start()

    def out_last():
        for k in range(1, 4):
            z = (z_at + k) % 4
            at = woall.at[x_at * 4 + z, 1 - core]
            remote(at, at, oss.at[0], osr.at[z], sibling, r).wait_recv()
            x = (x_at + k) % 4
            at = woall.at[pl.ds(4 * x, 4), 1 - core]
            remote(at, at, obs.at[0], obr.at[x], sibling, r).wait_recv()

    def out_sent():
        for k in range(1, 4):
            out_z(k).wait_send()
            out_x(k).wait_send()
            out_z_sibling(k).wait_send()
            out_x_sibling(k).wait_send()

    pl.semaphore_wait(entered, N - 1)
    loop(0, 8, pos_start)
    loop(1, N, lambda k: p1_in((i + k) % N).wait_recv())
    for t in range(N):
        fwd[t] = in1[owners[t], ranks[t]]

    def p2(t):
        tile, seq = worker(t, r8, y_at, z_low)
        return remote(
            fwd.at[t], pix.at[core, rm], p2s.at[t], p2r.at[core * 8 + rm], tile, seq
        )

    home_tile, home_seq = worker(my_tile, r8, y_at, z_low)
    away = (home_tile != i) | (home_seq != r)
    loop(1, N, lambda k: p2((my_tile + k) % N).start())

    @pl.when(away)
    def _():
        p2(my_tile).start()

    @pl.when(jnp.logical_not(away))
    def _():
        pix[core, rm] = fwd[my_tile]

    out_own()

    for f in range(2):
        source = 2 * kc_mine + f

        def p2_in(k, f=f, source=source):
            @pl.when((source != i) | (upper * 8 + k != r))
            def _():
                remote(
                    fwd.at[0], pix.at[f, k], p2s.at[0], p2r.at[f * 8 + k], i, r
                ).wait_recv()

        loop(0, 8, p2_in)

    def pos_in(k):
        @pl.when((upper * 8 + k != r) | (x_at % 2 == 1))
        def _():
            remote(pos.at[0], posall.at[k], pos_s.at[0], pos_r.at[k], i, r).wait_recv()

    loop(0, 8, pos_in)
    wqall[z_at] = wq[...]
    weights_copies[0].start()
    weights_copies[1].start()
    loads[0].wait()
    stream = dot(pix[0].reshape(128, FH), we[0:FH]) + dot(pix[1].reshape(128, FH), we[FH:PV])
    stream = stream + posall[...].reshape(128, D).astype(jnp.float32)
    x_ref[...] = stream
    nbuf[core] = layer_norm(stream, gains[0:1])
    sib = remote(nbuf.at[core], nbuf.at[core], sib_s, sib_r, sibling, r)
    sib.start()
    sib_in = remote(nbuf.at[1 - core], nbuf.at[1 - core], sib_s, sib_r, sibling, r)
    out_pass_z()
    loads[1].wait()
    sib_in.wait_recv()

    def window_heads(pair):
        columns = w1[:, pl.ds(pl.multiple_of(pair * 384, 384), 384)]
        mine = dot(nbuf[core], columns).astype(jnp.bfloat16)
        other = dot(nbuf[1 - core], columns).astype(jnp.bfloat16)
        both = jnp.concatenate([mine, other], axis=0)
        results = []
        for h in range(2):
            at = h * 192
            scores = lax.dot_general(
                mine[:, at : at + 64], both[:, at + 64 : at + 128], NT,
                preferred_element_type=jnp.float32,
            ) * HD ** (-0.5)
            top = jnp.max(scores, axis=-1, keepdims=True)
            weights = jnp.exp(scores - top)
            weights = weights / jnp.sum(weights, axis=-1, keepdims=True)
            results.append(dot(weights.astype(jnp.bfloat16), both[:, at + 128 : at + 192]))
        o1[:, pl.ds(pl.multiple_of(pair * 128, 128), 128)] = jnp.concatenate(
            results, axis=1
        ).astype(jnp.bfloat16)

    loop(0, 4, window_heads)
    pass_weights()
    loop(4, 8, window_heads)
    loads[2].wait()
    stream = x_ref[...] + dot(o1[...], wout[...])
    x_ref[...] = stream
    nall[x_at] = layer_norm(stream, gains[1:2])

    def tokens_x(k):
        at = nall.at[x_at]
        return remote(at, at, ns.at[k - 1], nr.at[x_at], i, ((x_at + k) % 4) * 4 + z_at)

    for k in (1, 3, 2):
        tokens_x(k).start()
    pass_weights_last()
    for k in range(1, 4):
        z = (z_at + k) % 4
        at = wqall.at[z, 1 - core]
        remote(at, at, qss.at[z], qsr.at[z], sibling, r).wait_recv()

    def to_head(x, k):
        quarter = (fourth + k) % 4
        at = q_out.at[x * 4 + quarter]
        return remote(
            at, q_in.at[x * 4 + fourth], as_.at[x * 4 + quarter], ar.at[x * 4 + fourth],
            member(quarter), r,
        )

    for step in (0, 1, 3, 2):
        x = (x_at + step) % 4
        if step > 0:
            at = nall.at[x]
            remote(at, at, ns.at[0], nr.at[x], i, r).wait_recv()
        tokens = nall[x]
        for k in (1, 2, 3, 0):
            quarter = (fourth + k) % 4
            found = lax.dot_general(
                wqall[quarter].reshape(192, D), tokens, NT, preferred_element_type=jnp.float32
            ).astype(jnp.bfloat16)
            if k > 0:
                q_out[x * 4 + quarter] = found
                to_head(x, k).start()
            else:
                q_in[x * 4 + fourth] = found

    def head_in(x):
        for k in range(1, 4):
            s = x * 4 + (fourth + k) % 4
            remote(q_out.at[s], q_in.at[s], as_.at[s], ar.at[s], i, r).wait_recv()

    out_pass_x()
    loop(0, 4, head_in)
    for s in range(N):
        at = s * 128
        qt[:, at : at + 128] = q_in[s, 0:64]
        kb[at : at + 128, :] = q_in[s, 64:128].astype(jnp.float32).T.astype(jnp.bfloat16)
        vt[:, at : at + 128] = q_in[s, 128:192]

    def home(j):
        return remote(
            o_out.at[j], o_in.at[my_head], bs.at[j], br.at[my_head],
            member(j % 4), (j // 4) * 4 + z_at,
        )

    def attend(k):
        b = (k + my_head // 2 + 1) % 8
        queries = qt[:, pl.ds(pl.multiple_of(b * 256, 256), 256)]
        scores = dot(kb[...], queries)
        top = jnp.max(scores, axis=0, keepdims=True)
        weights = jnp.exp2((scores - top) * (HD ** (-0.5) * 1.4426950408889634))
        total = jnp.sum(weights, axis=0, keepdims=True)
        mixed = (dot(vt[...], weights.astype(jnp.bfloat16)) / total).astype(jnp.bfloat16)
        o_out[2 * b] = mixed[:, 0:128]
        o_out[2 * b + 1] = mixed[:, 128:256]
        for e in range(2):
            j = 2 * b + e

            @pl.when(j != my_head)
            def _(j=j):
                home(j).start()

    loop(0, 8, attend)
    o_in[my_head] = o_out[my_head]
    out_last()

    def home_in(k):
        s = (my_head + k) % N
        remote(o_out.at[s], o_in.at[s], bs.at[s], br.at[s], i, r).wait_recv()

    loop(1, N, home_in)
    attended = o_in[...].reshape(D, 128).astype(jnp.float32).T.astype(jnp.bfloat16)
    stream = x_ref[...] + dot(attended, woall[...].reshape(D, D))
    loads[3].wait()
    logits = dot(layer_norm(stream, gains[2:3]), hw[...])
    lout[...] = logits.astype(jnp.bfloat16).reshape(8, 16, NCLS)

    collector = 2 * kc_mine + my_tile % 2

    def l1(k):
        return remote(
            lout.at[k], lin.at[my_tile // 2], l1s.at[k], l1r.at[my_tile // 2], collector, upper * 8 + k
        )

    def l1_start(k):
        away = (collector != i) | (upper * 8 + k != r)

        @pl.when(away)
        def _():
            l1(k).start()

        @pl.when(jnp.logical_not(away))
        def _():
            lin[my_tile // 2] = lout[k]

    loop(0, 8, l1_start)
    kc = i // 2

    def l1_in(k):
        giver, at = worker(2 * k + i % 2, r8, kc // 2, kc % 2)

        @pl.when((giver != i) | (at != r))
        def _():
            remote(lout.at[0], lin.at[k], l1s.at[0], l1r.at[k], i, r).wait_recv()

    slot = [owners[t] * MOST + ranks[t] for t in range(N)]
    lane = lax.broadcasted_iota(jnp.int32, (N * MOST * 16, 128), 1)
    line = lax.broadcasted_iota(jnp.int32, (N * MOST * 16, 128), 0)
    wanted = jnp.zeros((N * MOST * 16, 128), jnp.int32)
    for k in range(8):
        wanted = jnp.where(
            lane // 16 == k, jnp.where(core == 0, slot[2 * k], slot[2 * k + 1]), wanted
        )
    route = jnp.where(line == wanted * 16 + lane % 16, 1.0, 0.0).astype(jnp.bfloat16)
    loop(0, 8, l1_in)
    rout[...] = (
        dot(route, lin[...].reshape(128, NCLS)).astype(jnp.bfloat16).reshape(N, MOST, 16, NCLS)
    )

    def l2(s):
        return remote(rout.at[s], rin.at[i], l2s.at[s], l2r.at[i], s, r)

    loop(1, N, lambda k: l2((i + k) % N).start())
    rin[i] = rout[i]

    cell = lax.broadcasted_iota(jnp.int32, (2 * SC, 128), 0)
    token = lax.broadcasted_iota(jnp.int32, (2 * SC, 128), 1)
    t_row = (token // 8) % 2
    t_col = (token // 16) * 8 + token % 8
    c_row = jnp.where(cell >= SC, 1, 0)
    c_col = cell - SC * c_row
    count = jnp.zeros((2 * SC, 128), jnp.float32)
    spots = []
    for m in range(MOST):
        chosen = (c_row == t_row) & (c_col == t_col + begin[m])
        spots.append(jnp.where(chosen, 1.0, 0.0).astype(jnp.bfloat16))
        count = count + jnp.where((c_col >= begin[m]) & (c_col < begin[m] + 64), 1.0, 0.0)

    def l2_in(k):
        s = (i + k) % N
        remote(rout.at[s], rin.at[s], l2s.at[s], l2r.at[s], s, r).wait_recv()

    loop(1, N, l2_in)
    total = jnp.zeros((2 * SC, NCLS), jnp.float32)
    for m in range(MOST):
        pieces = [rin[2 * k, m] + rin[2 * k + 1, m] for k in range(8)]
        total = total + dot(spots[m], jnp.concatenate(pieces, axis=0))
    out_ref[...] = (total / jnp.maximum(count, 1.0)).reshape(2, SC, NCLS)

    loop(1, N, lambda k: p1((i + k) % N).wait_send())

    loop(0, 8, pos_sent)
    loop(1, N, lambda k: p2((my_tile + k) % N).wait_send())

    @pl.when(away)
    def _():
        p2(my_tile).wait_send()

    sib.wait_send()
    for k in range(1, 4):
        weights_sibling(k).wait_send()
        tokens_x(k).wait_send()
    for copy in weights_copies:
        copy.wait_send()
    out_sent()

    def heads_sent(x):
        for k in range(1, 4):
            to_head(x, k).wait_send()

    loop(0, 4, heads_sent)
    loop(1, N, lambda k: home((my_head + k) % N).wait_send())

    def l1_sent(k):
        @pl.when((collector != i) | (upper * 8 + k != r))
        def _():
            l1(k).wait_send()

    loop(0, 8, l1_sent)
    loop(1, N, lambda k: l2((i + k) % N).wait_send())


def local(
    scene_band, tile_list, embed_weight, position, norm_gains, window_qkv, window_out,
    global_qkv, global_out, head_weight,
):
    core = lax.axis_index("tile") % 2
    parts = position.reshape(2, 4, 2, 8, D)
    pos = lax.dynamic_index_in_dim(parts, core, 2, False).transpose(1, 0, 2, 3).reshape(4, 16, D)
    wq = global_qkv.T.reshape(2, 96, D)
    wo = global_out.reshape(2, 32, D)
    bf = jnp.bfloat16
    vmem = pl.BlockSpec(memory_space=pltpu.VMEM)
    hbm = pl.BlockSpec(memory_space=pl.ANY)
    dma = pltpu.SemaphoreType.DMA
    return pl.pallas_call(
        kernel,
        out_shape=jax.ShapeDtypeStruct((2, SC, NCLS), jnp.float32),
        in_specs=[hbm] + [vmem] * 5 + [hbm] * 4,
        out_specs=vmem,
        scratch_shapes=[
            pltpu.SMEM((N, 3), jnp.int32),
            pltpu.VMEM((PV, D), bf),
            pltpu.VMEM((D, 3 * D), bf),
            pltpu.VMEM((D, D), bf),
            pltpu.VMEM((D, NCLS), bf),
            dma((5,)),
            pltpu.VMEM((N, MOST, 16, FH), bf),
            pltpu.VMEM((N, MOST, 16, FH), bf),
            pltpu.VMEM((N, 16, FH), bf),
            pltpu.VMEM((2, 8, 16, FH), bf),
            pltpu.VMEM((8, 16, D), bf),
            pltpu.VMEM((2, 128, D), bf),
            pltpu.VMEM((128, D), jnp.float32),
            pltpu.VMEM((128, D), bf),
            pltpu.VMEM((4, 2, 96, D), bf),
            pltpu.VMEM((N, 2, 32, D), bf),
            pltpu.VMEM((N, 192, 128), bf),
            pltpu.VMEM((N, 192, 128), bf),
            pltpu.VMEM((64, 2048), bf),
            pltpu.VMEM((2048, 64), bf),
            pltpu.VMEM((64, 2048), bf),
            pltpu.VMEM((N, 64, 128), bf),
            pltpu.VMEM((N, 64, 128), bf),
            pltpu.VMEM((8, 16, NCLS), bf),
            pltpu.VMEM((8, 16, NCLS), bf),
            pltpu.VMEM((N, MOST, 16, NCLS), bf),
            pltpu.VMEM((N, MOST, 16, NCLS), bf),
            pltpu.VMEM((4, 128, D), bf),
            pltpu.SemaphoreType.REGULAR,
            dma((3,)), dma((4,)),
            dma((N,)), dma((N,)), dma((N,)), dma((N,)), dma((8,)), dma((8,)), dma, dma,
            dma((4,)), dma((4,)), dma((3, 4)), dma((4,)),
            dma((3,)), dma((3,)), dma((3,)), dma((3,)), dma((4,)), dma((4,)), dma((4,)), dma((4,)),
            dma((N,)), dma((N,)), dma((N,)), dma((N,)), dma((8,)), dma((8,)), dma((N,)), dma((N,)),
        ],
        compiler_params=pltpu.CompilerParams(
            collective_id=0, has_side_effects=True, vmem_limit_bytes=56 * 1024 * 1024
        ),
    )(
        tile_list, scene_band, pos, wq, wo, norm_gains,
        embed_weight, window_qkv, window_out, head_weight,
    )


def solution(mesh):
    return jax.shard_map(
        local,
        mesh=mesh,
        in_specs=(
            P("seq", "tile", None), P(), P(), P("seq", None), P(), P(), P(),
            P(None, "seq"), P("seq", None), P(),
        ),
        out_specs=P("seq", "tile", None),
        check_vma=False,
    )
```

```python
import functools
import jax
import jax.numpy as jnp
from jax import lax
from jax.experimental import pallas as pl
from jax.experimental.pallas import tpu as pltpu
from jax.sharding import PartitionSpec as P

D = 1024
HD = 64
PADMAX = 16
MOST = 3
N = 16
SC = 96
PV = 768
FH = 384
NCLS = 128
EPSILON = 1e-06
FAR = 4096
SCALE = HD ** (-0.5) * 1.4426950408889634
NT = (((1,), (1,)), ((), ()))


def layer_norm(stream, gain):
    centre = stream - jnp.mean(stream, axis=-1, keepdims=True)
    spread = jnp.mean(centre * centre, axis=-1, keepdims=True)
    return (centre * lax.rsqrt(spread + EPSILON) * gain).astype(jnp.bfloat16)


def dot(a, b):
    return jnp.dot(a, b, preferred_element_type=jnp.float32)


def remote(src, dst, send_sem, recv_sem, tile, seq):
    return pltpu.make_async_remote_copy(
        src_ref=src, dst_ref=dst, send_sem=send_sem, recv_sem=recv_sem,
        device_id=(tile, seq), device_id_type=pl.DeviceIdType.MESH,
    )


def loop(low, high, body):
    def step(k, carry):
        body(k)
        return carry

    lax.fori_loop(low, high, step, 0)


def kernel(
    tl_hbm, strip, pos, wq, wo, gains, we_hbm, w1_hbm, wout_hbm, hw_hbm, out_ref,
    tl, we, w1, wout, hw, load_sem,
    out1, in1, fwd, pix, posall, nbuf, x_ref, o1,
    wqall, woall, q_out, q_in, qt, kb, vt, o_out, o_in,
    lout, lin, rout, rin,
    nall, entered, ns, nr,
    p1s, p1r, p2s, p2r, pos_s, pos_r, sib_s, sib_r,
    qzs, qss, qr, qsr, ozs, oxs, oss, obs, ozr, oxr, osr, obr,
    as_, ar, bs, br, l1s, l1r, l2s, l2r,
):
    i = lax.axis_index("tile")
    r = lax.axis_index("seq")
    core = i % 2
    sibling = i + 1 - 2 * core
    x_at = r // 4
    z_at = r % 4
    y_at = i // 4
    z_low = (i % 4) // 2
    y_high = y_at // 2
    upper = y_at % 2
    kc_mine = 2 * x_at + core
    my_tile = z_at * 4 + z_low * 2 + y_high
    fourth = upper * 2 + core
    my_head = x_at * 4 + fourth
    r8 = r // 8
    rm = r % 8

    def worker(t, a, b, half):
        return ((t % 2) * 2 + a) * 4 + ((t // 2) % 2) * 2 + half, b * 4 + t // 4

    def member(quarter):
        return (y_high * 2 + quarter // 2) * 4 + z_low * 2 + quarter % 2

    loads = [
        pltpu.make_async_copy(we_hbm, we, load_sem.at[0]),
        pltpu.make_async_copy(w1_hbm, w1, load_sem.at[1]),
        pltpu.make_async_copy(wout_hbm, wout, load_sem.at[2]),
        pltpu.make_async_copy(hw_hbm, hw, load_sem.at[3]),
        pltpu.make_async_copy(tl_hbm, tl, load_sem.at[4]),
    ]
    for load in loads:
        load.start()

    barrier = pltpu.get_barrier_semaphore()

    def greet(k):
        pl.semaphore_signal(
            barrier, inc=1, device_id=((i + k) % N, r), device_id_type=pl.DeviceIdType.MESH
        )
        pl.semaphore_signal(
            barrier, inc=1, device_id=(i, (r + k) % N), device_id_type=pl.DeviceIdType.MESH
        )

    loop(1, N, greet)

    loads[4].wait()
    owners = [tl[t, 0] for t in range(N)]
    starts = [tl[t, 1] - tl[t, 2] for t in range(N)]
    ranks = []
    for t in range(N):
        rank = jnp.int32(0)
        for u in range(t):
            rank = rank + jnp.where(owners[u] == owners[t], 1, 0)
        ranks.append(jnp.minimum(rank, MOST - 1))
    begin = []
    for m in range(MOST):
        value = jnp.int32(FAR)
        for t in range(N):
            value = jnp.where((owners[t] == i) & (ranks[t] == m), starts[t], value)
        begin.append(value)

    cells = strip[...].reshape(2 * SC, PV)
    token = lax.broadcasted_iota(jnp.int32, (128, 2 * SC), 0)
    cell = lax.broadcasted_iota(jnp.int32, (128, 2 * SC), 1)
    t_row = (token // 8) % 2
    t_col = (token // 16) * 8 + token % 8
    c_row = jnp.where(cell >= SC, 1, 0)
    c_col = cell - SC * c_row
    for m in range(MOST):
        chosen = (c_row == t_row) & (c_col == t_col + begin[m])
        block = dot(jnp.where(chosen, 1.0, 0.0).astype(jnp.bfloat16), cells).astype(jnp.bfloat16)
        for c in range(N):
            k, f = c // 2, c % 2
            out1[c, m] = block[k * 16 : k * 16 + 16, f * FH : f * FH + FH]

    pl.semaphore_wait(barrier, 2 * (N - 1))

    def p1(c):
        return remote(out1.at[c], in1.at[i], p1s.at[c], p1r.at[i], c, r)

    def p1_in(s):
        return remote(out1.at[s], in1.at[s], p1s.at[s], p1r.at[s], s, r)

    loop(1, N, lambda k: p1((i + k) % N).start())
    in1[i] = out1[i]

    def greet_again(k):
        pl.semaphore_signal(
            entered, inc=1, device_id=(i, (r + k) % N), device_id_type=pl.DeviceIdType.MESH
        )

    loop(1, N, greet_again)

    aside = jnp.where(upper == r8, 0, 1)

    def pos_copy(n):
        to = 2 * (n // 4) + aside
        return remote(
            pos.at[to], posall.at[rm], pos_s.at[n], pos_r.at[rm],
            i + aside * (4 - 8 * upper), to * 4 + n % 4,
        )

    def pos_stays(n):
        return (aside == 0) & ((2 * (n // 4)) * 4 + n % 4 == r)

    def pos_start(n):
        @pl.when(jnp.logical_not(pos_stays(n)))
        def _():
            pos_copy(n).start()

        @pl.when(pos_stays(n))
        def _():
            posall[rm] = pos[x_at]

    def pos_sent(n):
        @pl.when(jnp.logical_not(pos_stays(n)))
        def _():
            pos_copy(n).wait_send()

    def place(dx, dz):
        return ((x_at + dx) % 4) * 4 + (z_at + dz) % 4

    def weights_at(z, part):
        if part == 2:
            return wqall.at[z % 4, core]
        return wqall.at[z % 4, core, pl.ds(part * 48, 48)]

    def weights_z(step, part, z, number):
        at = weights_at(z, part)
        return remote(
            at, at, qzs.at[number], qr.at[part, z % 4], i, x_at * 4 + (z_at + step) % 4
        )

    weights_copies = [
        weights_z(1, 2, z_at, 0),
        weights_z(3, 2, z_at, 1),
        weights_z(1, 0, z_at + 3, 2),
        weights_z(3, 1, z_at + 1, 3),
    ]

    def weights_in(z, part):
        at = weights_at(z, part)
        remote(at, at, qzs.at[0], qr.at[part, z % 4], i, r).wait_recv()

    def weights_sibling(k):
        z = (z_at + k) % 4
        at = wqall.at[z, core]
        return remote(at, at, qss.at[z], qsr.at[z], sibling, r)

    def pass_weights():
        weights_in(z_at + 3, 2)
        weights_copies[2].start()
        weights_sibling(3).start()
        weights_in(z_at + 1, 2)
        weights_copies[3].start()
        weights_sibling(1).start()

    def pass_weights_last():
        weights_in(z_at + 2, 0)
        weights_in(z_at + 2, 1)
        weights_sibling(2).start()

    def out_z(k):
        return remote(
            wo.at[core], woall.at[r, core], ozs.at[k - 1], ozr.at[z_at],
            i, x_at * 4 + (z_at + k) % 4,
        )

    def out_z_sibling(k):
        z = (z_at + k) % 4
        at = woall.at[x_at * 4 + z, core]
        return remote(at, at, oss.at[k - 1], osr.at[z], sibling, r)

    def out_x(k):
        at = woall.at[pl.ds(4 * x_at, 4), core]
        return remote(at, at, oxs.at[k - 1], oxr.at[x_at], i, ((x_at + k) % 4) * 4 + z_at)

    def out_x_sibling(k):
        x = (x_at + k) % 4
        at = woall.at[pl.ds(4 * x, 4), core]
        return remote(at, at, obs.at[k - 1], obr.at[x], sibling, r)

    def out_own():
        woall[r] = wo[...]
        for k in range(1, 4):
            out_z(k).start()

    def out_pass_z():
        for k in range(1, 4):
            z = (z_at + k) % 4
            remote(
                wo.at[core], woall.at[x_at * 4 + z, core], ozs.at[0], ozr.at[z], i, r
            ).wait_recv()
        for k in (1, 3, 2):
            out_x(k).start()
        for k in range(1, 4):
            out_z_sibling(k).start()

    def out_pass_x():
        for k in (1, 3, 2):
            x = (x_at + k) % 4
            at = woall.at[pl.ds(4 * x, 4), core]
            remote(at, at, oxs.at[0], oxr.at[x], i, r).wait_recv()
            out_x_sibling(k).start()

    def out_last():
        for k in range(1, 4):
            z = (z_at + k) % 4
            at = woall.at[x_at * 4 + z, 1 - core]
            remote(at, at, oss.at[0], osr.at[z], sibling, r).wait_recv()
            x = (x_at + k) % 4
            at = woall.at[pl.ds(4 * x, 4), 1 - core]
            remote(at, at, obs.at[0], obr.at[x], sibling, r).wait_recv()

    def out_sent():
        for k in range(1, 4):
            out_z(k).wait_send()
            out_x(k).wait_send()
            out_z_sibling(k).wait_send()
            out_x_sibling(k).wait_send()

    pl.semaphore_wait(entered, N - 1)
    loop(0, 8, pos_start)
    loop(1, N, lambda k: p1_in((i + k) % N).wait_recv())
    for t in range(N):
        fwd[t] = in1[owners[t], ranks[t]]

    def p2(t):
        tile, seq = worker(t, r8, y_at, z_low)
        return remote(
            fwd.at[t], pix.at[core, rm], p2s.at[t], p2r.at[core * 8 + rm], tile, seq
        )

    home_tile, home_seq = worker(my_tile, r8, y_at, z_low)
    away = (home_tile != i) | (home_seq != r)
    loop(1, N, lambda k: p2((my_tile + k) % N).start())

    @pl.when(away)
    def _():
        p2(my_tile).start()

    @pl.when(jnp.logical_not(away))
    def _():
        pix[core, rm] = fwd[my_tile]

    out_own()

    for f in range(2):
        source = 2 * kc_mine + f

        def p2_in(k, f=f, source=source):
            @pl.when((source != i) | (upper * 8 + k != r))
            def _():
                remote(
                    fwd.at[0], pix.at[f, k], p2s.at[0], p2r.at[f * 8 + k], i, r
                ).wait_recv()

        loop(0, 8, p2_in)

    def pos_in(k):
        @pl.when((upper * 8 + k != r) | (x_at % 2 == 1))
        def _():
            remote(pos.at[0], posall.at[k], pos_s.at[0], pos_r.at[k], i, r).wait_recv()

    loop(0, 8, pos_in)
    wqall[z_at] = wq[...]
    weights_copies[0].start()
    weights_copies[1].start()
    loads[0].wait()
    stream = dot(pix[0].reshape(128, FH), we[0:FH]) + dot(pix[1].reshape(128, FH), we[FH:PV])
    stream = stream + posall[...].reshape(128, D).astype(jnp.float32)
    x_ref[...] = stream
    nbuf[core] = layer_norm(stream, gains[0:1])
    sib = remote(nbuf.at[core], nbuf.at[core], sib_s, sib_r, sibling, r)
    sib.start()
    sib_in = remote(nbuf.at[1 - core], nbuf.at[1 - core], sib_s, sib_r, sibling, r)
    out_pass_z()
    loads[1].wait()
    sib_in.wait_recv()

    def window_heads(quad):
        columns = w1[:, pl.ds(pl.multiple_of(quad * 768, 768), 768)]
        both = dot(nbuf[...].reshape(256, D), columns).astype(jnp.bfloat16)
        scores = []
        for h in range(4):
            at = h * 192
            mine = jnp.where(core == 0, both[:128, at : at + 64], both[128:, at : at + 64])
            scores.append(
                lax.dot_general(
                    mine, both[:, at + 64 : at + 128], NT, preferred_element_type=jnp.float32
                )
            )
        results = []
        for h in range(4):
            at = h * 192
            top = jnp.max(scores[h], axis=-1, keepdims=True)
            weights = jnp.exp2((scores[h] - top) * SCALE)
            total = jnp.sum(weights, axis=-1, keepdims=True)
            mixed = dot(weights.astype(jnp.bfloat16), both[:, at + 128 : at + 192])
            results.append(mixed / total)
        o1[:, pl.ds(pl.multiple_of(quad * 256, 256), 256)] = jnp.concatenate(
            results, axis=1
        ).astype(jnp.bfloat16)

    loop(0, 2, window_heads)
    pass_weights()
    loop(2, 4, window_heads)
    loads[2].wait()
    stream = x_ref[...] + dot(o1[...], wout[...])
    x_ref[...] = stream
    nall[x_at] = layer_norm(stream, gains[1:2])

    def tokens_x(k):
        at = nall.at[x_at]
        return remote(at, at, ns.at[k - 1], nr.at[x_at], i, ((x_at + k) % 4) * 4 + z_at)

    for k in (1, 3, 2):
        tokens_x(k).start()
    pass_weights_last()
    for k in range(1, 4):
        z = (z_at + k) % 4
        at = wqall.at[z, 1 - core]
        remote(at, at, qss.at[z], qsr.at[z], sibling, r).wait_recv()

    def to_head(x, k):
        quarter = (fourth + k) % 4
        at = q_out.at[x * 4 + quarter]
        return remote(
            at, q_in.at[x * 4 + fourth], as_.at[x * 4 + quarter], ar.at[x * 4 + fourth],
            member(quarter), r,
        )

    for step in (0, 1, 3, 2):
        x = (x_at + step) % 4
        if step > 0:
            at = nall.at[x]
            remote(at, at, ns.at[0], nr.at[x], i, r).wait_recv()
        tokens = nall[x]
        for k in (1, 2, 3, 0):
            quarter = (fourth + k) % 4
            found = lax.dot_general(
                wqall[quarter].reshape(192, D), tokens, NT, preferred_element_type=jnp.float32
            ).astype(jnp.bfloat16)
            if k > 0:
                q_out[x * 4 + quarter] = found
                to_head(x, k).start()
            else:
                q_in[x * 4 + fourth] = found

    def head_in(x):
        for k in range(1, 4):
            s = x * 4 + (fourth + k) % 4
            remote(q_out.at[s], q_in.at[s], as_.at[s], ar.at[s], i, r).wait_recv()

    out_pass_x()
    loop(0, 4, head_in)
    for s in range(N):
        at = s * 128
        qt[:, at : at + 128] = q_in[s, 0:64]
        kb[at : at + 128, :] = q_in[s, 64:128].astype(jnp.float32).T.astype(jnp.bfloat16)
        vt[:, at : at + 128] = q_in[s, 128:192]

    def home(j):
        return remote(
            o_out.at[j], o_in.at[my_head], bs.at[j], br.at[my_head],
            member(j % 4), (j // 4) * 4 + z_at,
        )

    def attend(k):
        blocks = [(2 * k + e + my_head // 2 + 1) % 8 for e in range(2)]
        scores = [
            dot(kb[...], qt[:, pl.ds(pl.multiple_of(b * 256, 256), 256)]) for b in blocks
        ]
        for b, score in zip(blocks, scores):
            top = jnp.max(score, axis=0, keepdims=True)
            weights = jnp.exp2((score - top) * SCALE)
            total = jnp.sum(weights, axis=0, keepdims=True)
            mixed = (dot(vt[...], weights.astype(jnp.bfloat16)) / total).astype(jnp.bfloat16)
            for e in range(2):
                j = 2 * b + e
                o_out[j] = mixed[:, 128 * e : 128 * e + 128]

                @pl.when(j != my_head)
                def _(j=j):
                    home(j).start()

    loop(0, 4, attend)
    o_in[my_head] = o_out[my_head]
    out_last()

    def home_in(k):
        s = (my_head + k) % N
        remote(o_out.at[s], o_in.at[s], bs.at[s], br.at[s], i, r).wait_recv()

    loop(1, N, home_in)
    attended = o_in[...].reshape(D, 128).astype(jnp.float32).T.astype(jnp.bfloat16)
    stream = x_ref[...] + dot(attended, woall[...].reshape(D, D))
    loads[3].wait()
    logits = dot(layer_norm(stream, gains[2:3]), hw[...])
    lout[...] = logits.astype(jnp.bfloat16).reshape(8, 16, NCLS)

    collector = 2 * kc_mine + my_tile % 2

    def l1(k):
        return remote(
            lout.at[k], lin.at[my_tile // 2], l1s.at[k], l1r.at[my_tile // 2], collector, upper * 8 + k
        )

    def l1_start(k):
        away = (collector != i) | (upper * 8 + k != r)

        @pl.when(away)
        def _():
            l1(k).start()

        @pl.when(jnp.logical_not(away))
        def _():
            lin[my_tile // 2] = lout[k]

    loop(0, 8, l1_start)
    kc = i // 2

    def l1_in(k):
        giver, at = worker(2 * k + i % 2, r8, kc // 2, kc % 2)

        @pl.when((giver != i) | (at != r))
        def _():
            remote(lout.at[0], lin.at[k], l1s.at[0], l1r.at[k], i, r).wait_recv()

    slot = [owners[t] * MOST + ranks[t] for t in range(N)]
    lane = lax.broadcasted_iota(jnp.int32, (N * MOST * 16, 128), 1)
    line = lax.broadcasted_iota(jnp.int32, (N * MOST * 16, 128), 0)
    wanted = jnp.zeros((N * MOST * 16, 128), jnp.int32)
    for k in range(8):
        wanted = jnp.where(
            lane // 16 == k, jnp.where(core == 0, slot[2 * k], slot[2 * k + 1]), wanted
        )
    route = jnp.where(line == wanted * 16 + lane % 16, 1.0, 0.0).astype(jnp.bfloat16)
    loop(0, 8, l1_in)
    rout[...] = (
        dot(route, lin[...].reshape(128, NCLS)).astype(jnp.bfloat16).reshape(N, MOST, 16, NCLS)
    )

    def l2(s):
        return remote(rout.at[s], rin.at[i], l2s.at[s], l2r.at[i], s, r)

    loop(1, N, lambda k: l2((i + k) % N).start())
    rin[i] = rout[i]

    cell = lax.broadcasted_iota(jnp.int32, (2 * SC, 128), 0)
    token = lax.broadcasted_iota(jnp.int32, (2 * SC, 128), 1)
    t_row = (token // 8) % 2
    t_col = (token // 16) * 8 + token % 8
    c_row = jnp.where(cell >= SC, 1, 0)
    c_col = cell - SC * c_row
    count = jnp.zeros((2 * SC, 128), jnp.float32)
    spots = []
    for m in range(MOST):
        chosen = (c_row == t_row) & (c_col == t_col + begin[m])
        spots.append(jnp.where(chosen, 1.0, 0.0).astype(jnp.bfloat16))
        count = count + jnp.where((c_col >= begin[m]) & (c_col < begin[m] + 64), 1.0, 0.0)

    def l2_in(k):
        s = (i + k) % N
        remote(rout.at[s], rin.at[s], l2s.at[s], l2r.at[s], s, r).wait_recv()

    loop(1, N, l2_in)
    total = jnp.zeros((2 * SC, NCLS), jnp.float32)
    for m in range(MOST):
        pieces = [rin[2 * k, m] + rin[2 * k + 1, m] for k in range(8)]
        total = total + dot(spots[m], jnp.concatenate(pieces, axis=0))
    out_ref[...] = (total / jnp.maximum(count, 1.0)).reshape(2, SC, NCLS)

    loop(1, N, lambda k: p1((i + k) % N).wait_send())

    loop(0, 8, pos_sent)
    loop(1, N, lambda k: p2((my_tile + k) % N).wait_send())

    @pl.when(away)
    def _():
        p2(my_tile).wait_send()

    sib.wait_send()
    for k in range(1, 4):
        weights_sibling(k).wait_send()
        tokens_x(k).wait_send()
    for copy in weights_copies:
        copy.wait_send()
    out_sent()

    def heads_sent(x):
        for k in range(1, 4):
            to_head(x, k).wait_send()

    loop(0, 4, heads_sent)
    loop(1, N, lambda k: home((my_head + k) % N).wait_send())

    def l1_sent(k):
        @pl.when((collector != i) | (upper * 8 + k != r))
        def _():
            l1(k).wait_send()

    loop(0, 8, l1_sent)
    loop(1, N, lambda k: l2((i + k) % N).wait_send())


def local(
    scene_band, tile_list, embed_weight, position, norm_gains, window_qkv, window_out,
    global_qkv, global_out, head_weight,
):
    core = lax.axis_index("tile") % 2
    parts = position.reshape(2, 4, 2, 8, D)
    pos = lax.dynamic_index_in_dim(parts, core, 2, False).transpose(1, 0, 2, 3).reshape(4, 16, D)
    wq = global_qkv.T.reshape(2, 96, D)
    wo = global_out.reshape(2, 32, D)
    bf = jnp.bfloat16
    vmem = pl.BlockSpec(memory_space=pltpu.VMEM)
    hbm = pl.BlockSpec(memory_space=pl.ANY)
    dma = pltpu.SemaphoreType.DMA
    return pl.pallas_call(
        kernel,
        out_shape=jax.ShapeDtypeStruct((2, SC, NCLS), jnp.float32),
        in_specs=[hbm] + [vmem] * 5 + [hbm] * 4,
        out_specs=vmem,
        scratch_shapes=[
            pltpu.SMEM((N, 3), jnp.int32),
            pltpu.VMEM((PV, D), bf),
            pltpu.VMEM((D, 3 * D), bf),
            pltpu.VMEM((D, D), bf),
            pltpu.VMEM((D, NCLS), bf),
            dma((5,)),
            pltpu.VMEM((N, MOST, 16, FH), bf),
            pltpu.VMEM((N, MOST, 16, FH), bf),
            pltpu.VMEM((N, 16, FH), bf),
            pltpu.VMEM((2, 8, 16, FH), bf),
            pltpu.VMEM((8, 16, D), bf),
            pltpu.VMEM((2, 128, D), bf),
            pltpu.VMEM((128, D), jnp.float32),
            pltpu.VMEM((128, D), bf),
            pltpu.VMEM((4, 2, 96, D), bf),
            pltpu.VMEM((N, 2, 32, D), bf),
            pltpu.VMEM((N, 192, 128), bf),
            pltpu.VMEM((N, 192, 128), bf),
            pltpu.VMEM((64, 2048), bf),
            pltpu.VMEM((2048, 64), bf),
            pltpu.VMEM((64, 2048), bf),
            pltpu.VMEM((N, 64, 128), bf),
            pltpu.VMEM((N, 64, 128), bf),
            pltpu.VMEM((8, 16, NCLS), bf),
            pltpu.VMEM((8, 16, NCLS), bf),
            pltpu.VMEM((N, MOST, 16, NCLS), bf),
            pltpu.VMEM((N, MOST, 16, NCLS), bf),
            pltpu.VMEM((4, 128, D), bf),
            pltpu.SemaphoreType.REGULAR,
            dma((3,)), dma((4,)),
            dma((N,)), dma((N,)), dma((N,)), dma((N,)), dma((8,)), dma((8,)), dma, dma,
            dma((4,)), dma((4,)), dma((3, 4)), dma((4,)),
            dma((3,)), dma((3,)), dma((3,)), dma((3,)), dma((4,)), dma((4,)), dma((4,)), dma((4,)),
            dma((N,)), dma((N,)), dma((N,)), dma((N,)), dma((8,)), dma((8,)), dma((N,)), dma((N,)),
        ],
        compiler_params=pltpu.CompilerParams(
            collective_id=0, has_side_effects=True, vmem_limit_bytes=56 * 1024 * 1024
        ),
    )(
        tile_list, scene_band, pos, wq, wo, norm_gains,
        embed_weight, window_qkv, window_out, head_weight,
    )


def solution(mesh):
    return jax.shard_map(
        local,
        mesh=mesh,
        in_specs=(
            P("seq", "tile", None), P(), P(), P("seq", None), P(), P(), P(),
            P(None, "seq"), P("seq", None), P(),
        ),
        out_specs=P("seq", "tile", None),
        check_vma=False,
    )
```

```python
import functools
import jax
import jax.numpy as jnp
from jax import lax
from jax.experimental import pallas as pl
from jax.experimental.pallas import tpu as pltpu
from jax.sharding import PartitionSpec as P

D = 1024
HD = 64
PADMAX = 16
MOST = 3
N = 16
SC = 96
PV = 768
FH = 384
NCLS = 128
EPSILON = 1e-06
FAR = 4096
SCALE = HD ** (-0.5) * 1.4426950408889634
NT = (((1,), (1,)), ((), ()))


def layer_norm(stream, gain):
    centre = stream - jnp.mean(stream, axis=-1, keepdims=True)
    spread = jnp.mean(centre * centre, axis=-1, keepdims=True)
    return (centre * lax.rsqrt(spread + EPSILON) * gain).astype(jnp.bfloat16)


def dot(a, b):
    return jnp.dot(a, b, preferred_element_type=jnp.float32)


def remote(src, dst, send_sem, recv_sem, tile, seq):
    return pltpu.make_async_remote_copy(
        src_ref=src, dst_ref=dst, send_sem=send_sem, recv_sem=recv_sem,
        device_id=(tile, seq), device_id_type=pl.DeviceIdType.MESH,
    )


def loop(low, high, body):
    def step(k, carry):
        body(k)
        return carry

    lax.fori_loop(low, high, step, 0)


def kernel(
    tl_hbm, strip, pos, wq, wo, gains, we_hbm, w1_hbm, wout_hbm, hw_hbm, out_ref,
    tl, we, w1, wout, hw, load_sem,
    out1, in1, fwd, pix, posall, nbuf, x_ref, o1,
    wqall, woall, q_out, q_in, qt, kb, vt, o_out, o_in,
    lout, lin, rout, rin,
    nall, entered, ns, nr,
    p1s, p1r, p2s, p2r, pos_s, pos_r, sib_s, sib_r,
    qzs, qss, qr, qsr, ozs, oxs, oss, obs, ozr, oxr, osr, obr,
    as_, ar, bs, br, l1s, l1r, l2s, l2r,
):
    i = lax.axis_index("tile")
    r = lax.axis_index("seq")
    core = i % 2
    sibling = i + 1 - 2 * core
    x_at = r // 4
    z_at = r % 4
    y_at = i // 4
    z_low = (i % 4) // 2
    y_high = y_at // 2
    upper = y_at % 2
    kc_mine = 2 * x_at + core
    my_tile = z_at * 4 + z_low * 2 + y_high
    fourth = upper * 2 + core
    my_head = x_at * 4 + fourth
    r8 = r // 8
    rm = r % 8

    def worker(t, a, b, half):
        return ((t % 2) * 2 + a) * 4 + ((t // 2) % 2) * 2 + half, b * 4 + t // 4

    def member(quarter):
        return (y_high * 2 + quarter // 2) * 4 + z_low * 2 + quarter % 2

    loads = [
        pltpu.make_async_copy(we_hbm, we, load_sem.at[0]),
        pltpu.make_async_copy(w1_hbm, w1, load_sem.at[1]),
        pltpu.make_async_copy(wout_hbm, wout, load_sem.at[2]),
        pltpu.make_async_copy(hw_hbm, hw, load_sem.at[3]),
        pltpu.make_async_copy(tl_hbm, tl, load_sem.at[4]),
    ]
    for load in loads:
        load.start()

    barrier = pltpu.get_barrier_semaphore()

    def greet(k):
        pl.semaphore_signal(
            barrier, inc=1, device_id=((i + k) % N, r), device_id_type=pl.DeviceIdType.MESH
        )
        pl.semaphore_signal(
            barrier, inc=1, device_id=(i, (r + k) % N), device_id_type=pl.DeviceIdType.MESH
        )

    loop(1, N, greet)

    loads[4].wait()
    owners = [tl[0, t] for t in range(N)]
    starts = [tl[1, t] - tl[2, t] for t in range(N)]
    ranks = []
    for t in range(N):
        rank = jnp.int32(0)
        for u in range(t):
            rank = rank + jnp.where(owners[u] == owners[t], 1, 0)
        ranks.append(jnp.minimum(rank, MOST - 1))
    begin = []
    for m in range(MOST):
        value = jnp.int32(FAR)
        for t in range(N):
            value = jnp.where((owners[t] == i) & (ranks[t] == m), starts[t], value)
        begin.append(value)

    cells = strip[...].reshape(2 * SC, PV)
    token = lax.broadcasted_iota(jnp.int32, (128, 2 * SC), 0)
    cell = lax.broadcasted_iota(jnp.int32, (128, 2 * SC), 1)
    t_row = (token // 8) % 2
    t_col = (token // 16) * 8 + token % 8
    c_row = jnp.where(cell >= SC, 1, 0)
    c_col = cell - SC * c_row
    for m in range(MOST):
        chosen = (c_row == t_row) & (c_col == t_col + begin[m])
        block = dot(jnp.where(chosen, 1.0, 0.0).astype(jnp.bfloat16), cells).astype(jnp.bfloat16)
        for c in range(N):
            k, f = c // 2, c % 2
            out1[c, m] = block[k * 16 : k * 16 + 16, f * FH : f * FH + FH]

    pl.semaphore_wait(barrier, 2 * (N - 1))

    def p1(c):
        return remote(out1.at[c], in1.at[i], p1s.at[c], p1r.at[i], c, r)

    def p1_in(s):
        return remote(out1.at[s], in1.at[s], p1s.at[s], p1r.at[s], s, r)

    loop(1, N, lambda k: p1((i + k) % N).start())
    in1[i] = out1[i]

    def greet_again(k):
        pl.semaphore_signal(
            entered, inc=1, device_id=(i, (r + k) % N), device_id_type=pl.DeviceIdType.MESH
        )

    loop(1, N, greet_again)

    aside = jnp.where(upper == r8, 0, 1)

    def pos_copy(n):
        to = 2 * (n // 4) + aside
        return remote(
            pos.at[to], posall.at[rm], pos_s.at[n], pos_r.at[rm],
            i + aside * (4 - 8 * upper), to * 4 + n % 4,
        )

    def pos_stays(n):
        return (aside == 0) & ((2 * (n // 4)) * 4 + n % 4 == r)

    def pos_start(n):
        @pl.when(jnp.logical_not(pos_stays(n)))
        def _():
            pos_copy(n).start()

        @pl.when(pos_stays(n))
        def _():
            posall[rm] = pos[x_at]

    def pos_sent(n):
        @pl.when(jnp.logical_not(pos_stays(n)))
        def _():
            pos_copy(n).wait_send()

    def place(dx, dz):
        return ((x_at + dx) % 4) * 4 + (z_at + dz) % 4

    def weights_at(z, part):
        if part == 2:
            return wqall.at[z % 4, core]
        return wqall.at[z % 4, core, pl.ds(part * 48, 48)]

    def weights_z(step, part, z, number):
        at = weights_at(z, part)
        return remote(
            at, at, qzs.at[number], qr.at[part, z % 4], i, x_at * 4 + (z_at + step) % 4
        )

    weights_copies = [
        weights_z(1, 2, z_at, 0),
        weights_z(3, 2, z_at, 1),
        weights_z(1, 0, z_at + 3, 2),
        weights_z(3, 1, z_at + 1, 3),
    ]

    def weights_in(z, part):
        at = weights_at(z, part)
        remote(at, at, qzs.at[0], qr.at[part, z % 4], i, r).wait_recv()

    def weights_sibling(k):
        z = (z_at + k) % 4
        at = wqall.at[z, core]
        return remote(at, at, qss.at[z], qsr.at[z], sibling, r)

    def pass_weights():
        weights_in(z_at + 3, 2)
        weights_copies[2].start()
        weights_sibling(3).start()
        weights_in(z_at + 1, 2)
        weights_copies[3].start()
        weights_sibling(1).start()

    def pass_weights_last():
        weights_in(z_at + 2, 0)
        weights_in(z_at + 2, 1)
        weights_sibling(2).start()

    def out_z(k):
        return remote(
            wo.at[core], woall.at[r, core], ozs.at[k - 1], ozr.at[z_at],
            i, x_at * 4 + (z_at + k) % 4,
        )

    def out_z_sibling(k):
        z = (z_at + k) % 4
        at = woall.at[x_at * 4 + z, core]
        return remote(at, at, oss.at[k - 1], osr.at[z], sibling, r)

    def out_x(k):
        at = woall.at[pl.ds(4 * x_at, 4), core]
        return remote(at, at, oxs.at[k - 1], oxr.at[x_at], i, ((x_at + k) % 4) * 4 + z_at)

    def out_x_sibling(k):
        x = (x_at + k) % 4
        at = woall.at[pl.ds(4 * x, 4), core]
        return remote(at, at, obs.at[k - 1], obr.at[x], sibling, r)

    def out_own():
        woall[r] = wo[...]
        for k in range(1, 4):
            out_z(k).start()

    def out_pass_z():
        for k in range(1, 4):
            z = (z_at + k) % 4
            remote(
                wo.at[core], woall.at[x_at * 4 + z, core], ozs.at[0], ozr.at[z], i, r
            ).wait_recv()
        for k in (1, 3, 2):
            out_x(k).start()
        for k in range(1, 4):
            out_z_sibling(k).start()

    def out_pass_x():
        for k in (1, 3, 2):
            x = (x_at + k) % 4
            at = woall.at[pl.ds(4 * x, 4), core]
            remote(at, at, oxs.at[0], oxr.at[x], i, r).wait_recv()
            out_x_sibling(k).start()

    def out_last():
        for k in range(1, 4):
            z = (z_at + k) % 4
            at = woall.at[x_at * 4 + z, 1 - core]
            remote(at, at, oss.at[0], osr.at[z], sibling, r).wait_recv()
            x = (x_at + k) % 4
            at = woall.at[pl.ds(4 * x, 4), 1 - core]
            remote(at, at, obs.at[0], obr.at[x], sibling, r).wait_recv()

    def out_sent():
        for k in range(1, 4):
            out_z(k).wait_send()
            out_x(k).wait_send()
            out_z_sibling(k).wait_send()
            out_x_sibling(k).wait_send()

    pl.semaphore_wait(entered, N - 1)
    loop(0, 8, pos_start)
    loop(1, N, lambda k: p1_in((i + k) % N).wait_recv())
    for t in range(N):
        fwd[t] = in1[owners[t], ranks[t]]

    def p2(t):
        tile, seq = worker(t, r8, y_at, z_low)
        return remote(
            fwd.at[t], pix.at[core, rm], p2s.at[t], p2r.at[core * 8 + rm], tile, seq
        )

    home_tile, home_seq = worker(my_tile, r8, y_at, z_low)
    away = (home_tile != i) | (home_seq != r)
    loop(1, N, lambda k: p2((my_tile + k) % N).start())

    @pl.when(away)
    def _():
        p2(my_tile).start()

    @pl.when(jnp.logical_not(away))
    def _():
        pix[core, rm] = fwd[my_tile]

    out_own()

    for f in range(2):
        source = 2 * kc_mine + f

        def p2_in(k, f=f, source=source):
            @pl.when((source != i) | (upper * 8 + k != r))
            def _():
                remote(
                    fwd.at[0], pix.at[f, k], p2s.at[0], p2r.at[f * 8 + k], i, r
                ).wait_recv()

        loop(0, 8, p2_in)

    def pos_in(k):
        @pl.when((upper * 8 + k != r) | (x_at % 2 == 1))
        def _():
            remote(pos.at[0], posall.at[k], pos_s.at[0], pos_r.at[k], i, r).wait_recv()

    loop(0, 8, pos_in)
    wqall[z_at] = wq[...]
    weights_copies[0].start()
    weights_copies[1].start()
    loads[0].wait()
    stream = dot(pix[0].reshape(128, FH), we[0:FH]) + dot(pix[1].reshape(128, FH), we[FH:PV])
    stream = stream + posall[...].reshape(128, D).astype(jnp.float32)
    x_ref[...] = stream
    nbuf[core] = layer_norm(stream, gains[0:1])
    sib = remote(nbuf.at[core], nbuf.at[core], sib_s, sib_r, sibling, r)
    sib.start()
    sib_in = remote(nbuf.at[1 - core], nbuf.at[1 - core], sib_s, sib_r, sibling, r)
    out_pass_z()
    loads[1].wait()
    sib_in.wait_recv()

    def window_heads(quad):
        columns = w1[:, pl.ds(pl.multiple_of(quad * 768, 768), 768)]
        both = dot(nbuf[...].reshape(256, D), columns).astype(jnp.bfloat16)
        scores = []
        for h in range(4):
            at = h * 192
            mine = jnp.where(core == 0, both[:128, at : at + 64], both[128:, at : at + 64])
            scores.append(
                lax.dot_general(
                    mine, both[:, at + 64 : at + 128], NT, preferred_element_type=jnp.float32
                )
            )
        results = []
        for h in range(4):
            at = h * 192
            top = jnp.max(scores[h], axis=-1, keepdims=True)
            weights = jnp.exp2((scores[h] - top) * SCALE)
            total = jnp.sum(weights, axis=-1, keepdims=True)
            mixed = dot(weights.astype(jnp.bfloat16), both[:, at + 128 : at + 192])
            results.append(mixed / total)
        o1[:, pl.ds(pl.multiple_of(quad * 256, 256), 256)] = jnp.concatenate(
            results, axis=1
        ).astype(jnp.bfloat16)

    loop(0, 2, window_heads)
    pass_weights()
    loop(2, 4, window_heads)
    loads[2].wait()
    stream = x_ref[...] + dot(o1[...], wout[...])
    x_ref[...] = stream
    nall[x_at] = layer_norm(stream, gains[1:2])

    def tokens_x(k):
        at = nall.at[x_at]
        return remote(at, at, ns.at[k - 1], nr.at[x_at], i, ((x_at + k) % 4) * 4 + z_at)

    for k in (1, 3, 2):
        tokens_x(k).start()
    pass_weights_last()
    for k in range(1, 4):
        z = (z_at + k) % 4
        at = wqall.at[z, 1 - core]
        remote(at, at, qss.at[z], qsr.at[z], sibling, r).wait_recv()

    def to_head(x, k):
        quarter = (fourth + k) % 4
        at = q_out.at[x * 4 + quarter]
        return remote(
            at, q_in.at[x * 4 + fourth], as_.at[x * 4 + quarter], ar.at[x * 4 + fourth],
            member(quarter), r,
        )

    for step in (0, 1, 3, 2):
        x = (x_at + step) % 4
        if step > 0:
            at = nall.at[x]
            remote(at, at, ns.at[0], nr.at[x], i, r).wait_recv()
        tokens = nall[x]
        for k in (1, 2, 3, 0):
            quarter = (fourth + k) % 4
            found = lax.dot_general(
                wqall[quarter].reshape(192, D), tokens, NT, preferred_element_type=jnp.float32
            ).astype(jnp.bfloat16)
            if k > 0:
                q_out[x * 4 + quarter] = found
                to_head(x, k).start()
            else:
                q_in[x * 4 + fourth] = found

    def head_in(x):
        for k in range(1, 4):
            s = x * 4 + (fourth + k) % 4
            remote(q_out.at[s], q_in.at[s], as_.at[s], ar.at[s], i, r).wait_recv()

    out_pass_x()
    loop(0, 4, head_in)
    for s in range(N):
        at = s * 128
        qt[:, at : at + 128] = q_in[s, 0:64]
        kb[at : at + 128, :] = q_in[s, 64:128].astype(jnp.float32).T.astype(jnp.bfloat16)
        vt[:, at : at + 128] = q_in[s, 128:192]

    def home(j):
        return remote(
            o_out.at[j], o_in.at[my_head], bs.at[j], br.at[my_head],
            member(j % 4), (j // 4) * 4 + z_at,
        )

    def attend(k):
        blocks = [(2 * k + e + my_head // 2 + 1) % 8 for e in range(2)]
        scores = [
            dot(kb[...], qt[:, pl.ds(pl.multiple_of(b * 256, 256), 256)]) for b in blocks
        ]
        for b, score in zip(blocks, scores):
            top = jnp.max(score, axis=0, keepdims=True)
            weights = jnp.exp2((score - top) * SCALE)
            total = jnp.sum(weights, axis=0, keepdims=True)
            mixed = (dot(vt[...], weights.astype(jnp.bfloat16)) / total).astype(jnp.bfloat16)
            for e in range(2):
                j = 2 * b + e
                o_out[j] = mixed[:, 128 * e : 128 * e + 128]

                @pl.when(j != my_head)
                def _(j=j):
                    home(j).start()

    loop(0, 4, attend)
    o_in[my_head] = o_out[my_head]
    out_last()

    def home_in(k):
        s = (my_head + k) % N
        remote(o_out.at[s], o_in.at[s], bs.at[s], br.at[s], i, r).wait_recv()

    loop(1, N, home_in)
    attended = o_in[...].reshape(D, 128).astype(jnp.float32).T.astype(jnp.bfloat16)
    stream = x_ref[...] + dot(attended, woall[...].reshape(D, D))
    loads[3].wait()
    logits = dot(layer_norm(stream, gains[2:3]), hw[...])
    lout[...] = logits.astype(jnp.bfloat16).reshape(8, 16, NCLS)

    collector = 2 * kc_mine + my_tile % 2

    def l1(k):
        return remote(
            lout.at[k], lin.at[my_tile // 2], l1s.at[k], l1r.at[my_tile // 2], collector, upper * 8 + k
        )

    def l1_start(k):
        away = (collector != i) | (upper * 8 + k != r)

        @pl.when(away)
        def _():
            l1(k).start()

        @pl.when(jnp.logical_not(away))
        def _():
            lin[my_tile // 2] = lout[k]

    loop(0, 8, l1_start)
    kc = i // 2

    def l1_in(k):
        giver, at = worker(2 * k + i % 2, r8, kc // 2, kc % 2)

        @pl.when((giver != i) | (at != r))
        def _():
            remote(lout.at[0], lin.at[k], l1s.at[0], l1r.at[k], i, r).wait_recv()

    slot = [owners[t] * MOST + ranks[t] for t in range(N)]
    lane = lax.broadcasted_iota(jnp.int32, (N * MOST * 16, 128), 1)
    line = lax.broadcasted_iota(jnp.int32, (N * MOST * 16, 128), 0)
    wanted = jnp.zeros((N * MOST * 16, 128), jnp.int32)
    for k in range(8):
        wanted = jnp.where(
            lane // 16 == k, jnp.where(core == 0, slot[2 * k], slot[2 * k + 1]), wanted
        )
    route = jnp.where(line == wanted * 16 + lane % 16, 1.0, 0.0).astype(jnp.bfloat16)
    loop(0, 8, l1_in)
    rout[...] = (
        dot(route, lin[...].reshape(128, NCLS)).astype(jnp.bfloat16).reshape(N, MOST, 16, NCLS)
    )

    def l2(s):
        return remote(rout.at[s], rin.at[i], l2s.at[s], l2r.at[i], s, r)

    loop(1, N, lambda k: l2((i + k) % N).start())
    rin[i] = rout[i]

    cell = lax.broadcasted_iota(jnp.int32, (2 * SC, 128), 0)
    token = lax.broadcasted_iota(jnp.int32, (2 * SC, 128), 1)
    t_row = (token // 8) % 2
    t_col = (token // 16) * 8 + token % 8
    c_row = jnp.where(cell >= SC, 1, 0)
    c_col = cell - SC * c_row
    count = jnp.zeros((2 * SC, 128), jnp.float32)
    spots = []
    for m in range(MOST):
        chosen = (c_row == t_row) & (c_col == t_col + begin[m])
        spots.append(jnp.where(chosen, 1.0, 0.0).astype(jnp.bfloat16))
        count = count + jnp.where((c_col >= begin[m]) & (c_col < begin[m] + 64), 1.0, 0.0)

    def l2_in(k):
        s = (i + k) % N
        remote(rout.at[s], rin.at[s], l2s.at[s], l2r.at[s], s, r).wait_recv()

    loop(1, N, l2_in)
    total = jnp.zeros((2 * SC, NCLS), jnp.float32)
    for m in range(MOST):
        pieces = [rin[2 * k, m] + rin[2 * k + 1, m] for k in range(8)]
        total = total + dot(spots[m], jnp.concatenate(pieces, axis=0))
    out_ref[...] = (total / jnp.maximum(count, 1.0)).reshape(2, SC, NCLS)

    loop(1, N, lambda k: p1((i + k) % N).wait_send())

    loop(0, 8, pos_sent)
    loop(1, N, lambda k: p2((my_tile + k) % N).wait_send())

    @pl.when(away)
    def _():
        p2(my_tile).wait_send()

    sib.wait_send()
    for k in range(1, 4):
        weights_sibling(k).wait_send()
        tokens_x(k).wait_send()
    for copy in weights_copies:
        copy.wait_send()
    out_sent()

    def heads_sent(x):
        for k in range(1, 4):
            to_head(x, k).wait_send()

    loop(0, 4, heads_sent)
    loop(1, N, lambda k: home((my_head + k) % N).wait_send())

    def l1_sent(k):
        @pl.when((collector != i) | (upper * 8 + k != r))
        def _():
            l1(k).wait_send()

    loop(0, 8, l1_sent)
    loop(1, N, lambda k: l2((i + k) % N).wait_send())


def local(
    scene_band, tile_list, embed_weight, position, norm_gains, window_qkv, window_out,
    global_qkv, global_out, head_weight,
):
    core = lax.axis_index("tile") % 2
    parts = position.reshape(2, 4, 2, 8, D)
    pos = lax.dynamic_index_in_dim(parts, core, 2, False).transpose(1, 0, 2, 3).reshape(4, 16, D)
    wq = global_qkv.T.reshape(2, 96, D)
    wo = global_out.reshape(2, 32, D)
    bf = jnp.bfloat16
    vmem = pl.BlockSpec(memory_space=pltpu.VMEM)
    hbm = pl.BlockSpec(memory_space=pl.ANY)
    dma = pltpu.SemaphoreType.DMA
    return pl.pallas_call(
        kernel,
        out_shape=jax.ShapeDtypeStruct((2, SC, NCLS), jnp.float32),
        in_specs=[hbm] + [vmem] * 5 + [hbm] * 4,
        out_specs=vmem,
        scratch_shapes=[
            pltpu.SMEM((3, N), jnp.int32),
            pltpu.VMEM((PV, D), bf),
            pltpu.VMEM((D, 3 * D), bf),
            pltpu.VMEM((D, D), bf),
            pltpu.VMEM((D, NCLS), bf),
            dma((5,)),
            pltpu.VMEM((N, MOST, 16, FH), bf),
            pltpu.VMEM((N, MOST, 16, FH), bf),
            pltpu.VMEM((N, 16, FH), bf),
            pltpu.VMEM((2, 8, 16, FH), bf),
            pltpu.VMEM((8, 16, D), bf),
            pltpu.VMEM((2, 128, D), bf),
            pltpu.VMEM((128, D), jnp.float32),
            pltpu.VMEM((128, D), bf),
            pltpu.VMEM((4, 2, 96, D), bf),
            pltpu.VMEM((N, 2, 32, D), bf),
            pltpu.VMEM((N, 192, 128), bf),
            pltpu.VMEM((N, 192, 128), bf),
            pltpu.VMEM((64, 2048), bf),
            pltpu.VMEM((2048, 64), bf),
            pltpu.VMEM((64, 2048), bf),
            pltpu.VMEM((N, 64, 128), bf),
            pltpu.VMEM((N, 64, 128), bf),
            pltpu.VMEM((8, 16, NCLS), bf),
            pltpu.VMEM((8, 16, NCLS), bf),
            pltpu.VMEM((N, MOST, 16, NCLS), bf),
            pltpu.VMEM((N, MOST, 16, NCLS), bf),
            pltpu.VMEM((4, 128, D), bf),
            pltpu.SemaphoreType.REGULAR,
            dma((3,)), dma((4,)),
            dma((N,)), dma((N,)), dma((N,)), dma((N,)), dma((8,)), dma((8,)), dma, dma,
            dma((4,)), dma((4,)), dma((3, 4)), dma((4,)),
            dma((3,)), dma((3,)), dma((3,)), dma((3,)), dma((4,)), dma((4,)), dma((4,)), dma((4,)),
            dma((N,)), dma((N,)), dma((N,)), dma((N,)), dma((8,)), dma((8,)), dma((N,)), dma((N,)),
        ],
        compiler_params=pltpu.CompilerParams(
            collective_id=0, has_side_effects=True, vmem_limit_bytes=56 * 1024 * 1024
        ),
    )(
        tile_list.T, scene_band, pos, wq, wo, norm_gains,
        embed_weight, window_qkv, window_out, head_weight,
    )


def solution(mesh):
    return jax.shard_map(
        local,
        mesh=mesh,
        in_specs=(
            P("seq", "tile", None), P(), P(), P("seq", None), P(), P(), P(),
            P(None, "seq"), P("seq", None), P(),
        ),
        out_specs=P("seq", "tile", None),
        check_vma=False,
    )
```

```python
import functools
import jax
import jax.numpy as jnp
from jax import lax
from jax.experimental import pallas as pl
from jax.experimental.pallas import tpu as pltpu
from jax.sharding import PartitionSpec as P

D = 1024
HD = 64
PADMAX = 16
MOST = 3
N = 16
SC = 96
PV = 768
FH = 384
NCLS = 128
EPSILON = 1e-06
FAR = 4096
SCALE = HD ** (-0.5) * 1.4426950408889634
NT = (((1,), (1,)), ((), ()))


def layer_norm(stream, gain):
    centre = stream - jnp.mean(stream, axis=-1, keepdims=True)
    spread = jnp.mean(centre * centre, axis=-1, keepdims=True)
    return (centre * lax.rsqrt(spread + EPSILON) * gain).astype(jnp.bfloat16)


def dot(a, b):
    return jnp.dot(a, b, preferred_element_type=jnp.float32)


def remote(src, dst, send_sem, recv_sem, tile, seq):
    return pltpu.make_async_remote_copy(
        src_ref=src, dst_ref=dst, send_sem=send_sem, recv_sem=recv_sem,
        device_id=(tile, seq), device_id_type=pl.DeviceIdType.MESH,
    )


def loop(low, high, body):
    def step(k, carry):
        body(k)
        return carry

    lax.fori_loop(low, high, step, 0)


def kernel(
    tl_hbm, strip, pos, wq, wo, gains, we_hbm, w1_hbm, wout_hbm, hw_hbm, out_ref,
    tl, we, w1, wout, hw, load_sem,
    out1, in1, fwd, pix, posall, nbuf, x_ref, o1,
    wqall, woall, q_out, q_in, qt, kb, vt, o_out, o_in,
    lout, lin, rout, rin,
    nall, entered, ns, nr,
    p1s, p1r, p2s, p2r, pos_s, pos_r, sib_s, sib_r,
    qzs, qss, qr, qsr, ozs, oxs, oss, obs, ozr, oxr, osr, obr,
    as_, ar, bs, br, l1s, l1r, l2s, l2r,
):
    i = lax.axis_index("tile")
    r = lax.axis_index("seq")
    core = i % 2
    sibling = i + 1 - 2 * core
    x_at = r // 4
    z_at = r % 4
    y_at = i // 4
    z_low = (i % 4) // 2
    y_high = y_at // 2
    upper = y_at % 2
    kc_mine = 2 * x_at + core
    my_tile = z_at * 4 + z_low * 2 + y_high
    fourth = upper * 2 + core
    my_head = x_at * 4 + fourth
    r8 = r // 8
    rm = r % 8

    def worker(t, a, b, half):
        return ((t % 2) * 2 + a) * 4 + ((t // 2) % 2) * 2 + half, b * 4 + t // 4

    def member(quarter):
        return (y_high * 2 + quarter // 2) * 4 + z_low * 2 + quarter % 2

    loads = [
        pltpu.make_async_copy(we_hbm, we, load_sem.at[0]),
        pltpu.make_async_copy(w1_hbm, w1, load_sem.at[1]),
        pltpu.make_async_copy(wout_hbm, wout, load_sem.at[2]),
        pltpu.make_async_copy(hw_hbm, hw, load_sem.at[3]),
        pltpu.make_async_copy(tl_hbm, tl, load_sem.at[4]),
    ]
    for load in loads:
        load.start()

    barrier = pltpu.get_barrier_semaphore()

    def greet(k):
        pl.semaphore_signal(
            barrier, inc=1, device_id=((i + k) % N, r), device_id_type=pl.DeviceIdType.MESH
        )
        pl.semaphore_signal(
            barrier, inc=1, device_id=(i, (r + k) % N), device_id_type=pl.DeviceIdType.MESH
        )

    loop(1, N, greet)

    loads[4].wait()
    owners = [tl[0, t] for t in range(N)]
    starts = [tl[1, t] - tl[2, t] for t in range(N)]
    ranks = []
    for t in range(N):
        rank = jnp.int32(0)
        for u in range(t):
            rank = rank + jnp.where(owners[u] == owners[t], 1, 0)
        ranks.append(jnp.minimum(rank, MOST - 1))
    begin = []
    for m in range(MOST):
        value = jnp.int32(FAR)
        for t in range(N):
            value = jnp.where((owners[t] == i) & (ranks[t] == m), starts[t], value)
        begin.append(value)

    cells = strip[...].reshape(2 * SC, PV)
    token = lax.broadcasted_iota(jnp.int32, (128, 2 * SC), 0)
    cell = lax.broadcasted_iota(jnp.int32, (128, 2 * SC), 1)
    t_row = (token // 8) % 2
    t_col = (token // 16) * 8 + token % 8
    c_row = jnp.where(cell >= SC, 1, 0)
    c_col = cell - SC * c_row
    for m in range(MOST):
        chosen = (c_row == t_row) & (c_col == t_col + begin[m])
        block = dot(jnp.where(chosen, 1.0, 0.0).astype(jnp.bfloat16), cells).astype(jnp.bfloat16)
        for c in range(N):
            k, f = c // 2, c % 2
            out1[c, m] = block[k * 16 : k * 16 + 16, f * FH : f * FH + FH]

    pl.semaphore_wait(barrier, 2 * (N - 1))

    def p1(c):
        return remote(out1.at[c], in1.at[i], p1s.at[c], p1r.at[i], c, r)

    def p1_in(s):
        return remote(out1.at[s], in1.at[s], p1s.at[s], p1r.at[s], s, r)

    loop(1, N, lambda k: p1((i + k) % N).start())
    in1[i] = out1[i]

    def greet_again(k):
        pl.semaphore_signal(
            entered, inc=1, device_id=(i, (r + k) % N), device_id_type=pl.DeviceIdType.MESH
        )

    loop(1, N, greet_again)

    aside = jnp.where(upper == r8, 0, 1)

    def pos_copy(n):
        to = 2 * (n // 4) + aside
        return remote(
            pos.at[to], posall.at[rm], pos_s.at[n], pos_r.at[rm],
            i + aside * (4 - 8 * upper), to * 4 + n % 4,
        )

    def pos_stays(n):
        return (aside == 0) & ((2 * (n // 4)) * 4 + n % 4 == r)

    def pos_start(n):
        @pl.when(jnp.logical_not(pos_stays(n)))
        def _():
            pos_copy(n).start()

        @pl.when(pos_stays(n))
        def _():
            posall[rm] = pos[x_at]

    def pos_sent(n):
        @pl.when(jnp.logical_not(pos_stays(n)))
        def _():
            pos_copy(n).wait_send()

    def place(dx, dz):
        return ((x_at + dx) % 4) * 4 + (z_at + dz) % 4

    def weights_at(z, part):
        if part == 2:
            return wqall.at[z % 4, core]
        return wqall.at[z % 4, core, pl.ds(part * 48, 48)]

    def weights_z(step, part, z, number):
        at = weights_at(z, part)
        return remote(
            at, at, qzs.at[number], qr.at[part, z % 4], i, x_at * 4 + (z_at + step) % 4
        )

    weights_copies = [
        weights_z(1, 2, z_at, 0),
        weights_z(3, 2, z_at, 1),
        weights_z(1, 0, z_at + 3, 2),
        weights_z(3, 1, z_at + 1, 3),
    ]

    def weights_in(z, part):
        at = weights_at(z, part)
        remote(at, at, qzs.at[0], qr.at[part, z % 4], i, r).wait_recv()

    def weights_sibling(k):
        z = (z_at + k) % 4
        at = wqall.at[z, core]
        return remote(at, at, qss.at[z], qsr.at[z], sibling, r)

    def pass_weights():
        weights_in(z_at + 3, 2)
        weights_copies[2].start()
        weights_sibling(3).start()
        weights_in(z_at + 1, 2)
        weights_copies[3].start()
        weights_sibling(1).start()

    def pass_weights_last():
        weights_in(z_at + 2, 0)
        weights_in(z_at + 2, 1)
        weights_sibling(2).start()

    def out_z(k):
        return remote(
            wo.at[core], woall.at[r, core], ozs.at[k - 1], ozr.at[z_at],
            i, x_at * 4 + (z_at + k) % 4,
        )

    def out_z_sibling(k):
        z = (z_at + k) % 4
        at = woall.at[x_at * 4 + z, core]
        return remote(at, at, oss.at[k - 1], osr.at[z], sibling, r)

    def out_x(k):
        at = woall.at[pl.ds(4 * x_at, 4), core]
        return remote(at, at, oxs.at[k - 1], oxr.at[x_at], i, ((x_at + k) % 4) * 4 + z_at)

    def out_x_sibling(k):
        x = (x_at + k) % 4
        at = woall.at[pl.ds(4 * x, 4), core]
        return remote(at, at, obs.at[k - 1], obr.at[x], sibling, r)

    def out_own():
        woall[r] = wo[...]
        for k in range(1, 4):
            out_z(k).start()

    def out_pass_z():
        for k in range(1, 4):
            z = (z_at + k) % 4
            remote(
                wo.at[core], woall.at[x_at * 4 + z, core], ozs.at[0], ozr.at[z], i, r
            ).wait_recv()
        for k in (1, 3, 2):
            out_x(k).start()
        for k in range(1, 4):
            out_z_sibling(k).start()

    def out_pass_x():
        for k in (1, 3, 2):
            x = (x_at + k) % 4
            at = woall.at[pl.ds(4 * x, 4), core]
            remote(at, at, oxs.at[0], oxr.at[x], i, r).wait_recv()
            out_x_sibling(k).start()

    def out_last():
        for k in range(1, 4):
            z = (z_at + k) % 4
            at = woall.at[x_at * 4 + z, 1 - core]
            remote(at, at, oss.at[0], osr.at[z], sibling, r).wait_recv()
            x = (x_at + k) % 4
            at = woall.at[pl.ds(4 * x, 4), 1 - core]
            remote(at, at, obs.at[0], obr.at[x], sibling, r).wait_recv()

    def out_sent():
        for k in range(1, 4):
            out_z(k).wait_send()
            out_x(k).wait_send()
            out_z_sibling(k).wait_send()
            out_x_sibling(k).wait_send()

    pl.semaphore_wait(entered, N - 1)
    loop(0, 8, pos_start)
    loop(1, N, lambda k: p1_in((i + k) % N).wait_recv())
    for t in range(N):
        fwd[t] = in1[owners[t], ranks[t]]

    def p2(t):
        tile, seq = worker(t, r8, y_at, z_low)
        return remote(
            fwd.at[t], pix.at[core, rm], p2s.at[t], p2r.at[core * 8 + rm], tile, seq
        )

    home_tile, home_seq = worker(my_tile, r8, y_at, z_low)
    away = (home_tile != i) | (home_seq != r)
    loop(1, N, lambda k: p2((my_tile + k) % N).start())

    @pl.when(away)
    def _():
        p2(my_tile).start()

    @pl.when(jnp.logical_not(away))
    def _():
        pix[core, rm] = fwd[my_tile]

    out_own()

    for f in range(2):
        source = 2 * kc_mine + f

        def p2_in(k, f=f, source=source):
            @pl.when((source != i) | (upper * 8 + k != r))
            def _():
                remote(
                    fwd.at[0], pix.at[f, k], p2s.at[0], p2r.at[f * 8 + k], i, r
                ).wait_recv()

        loop(0, 8, p2_in)

    def pos_in(k):
        @pl.when((upper * 8 + k != r) | (x_at % 2 == 1))
        def _():
            remote(pos.at[0], posall.at[k], pos_s.at[0], pos_r.at[k], i, r).wait_recv()

    loop(0, 8, pos_in)
    wqall[z_at] = wq[...]
    weights_copies[0].start()
    weights_copies[1].start()
    loads[0].wait()
    stream = dot(pix[0].reshape(128, FH), we[0:FH]) + dot(pix[1].reshape(128, FH), we[FH:PV])
    stream = stream + posall[...].reshape(128, D).astype(jnp.float32)
    x_ref[...] = stream
    nbuf[core] = layer_norm(stream, gains[0:1])
    sib = remote(nbuf.at[core], nbuf.at[core], sib_s, sib_r, sibling, r)
    sib.start()
    sib_in = remote(nbuf.at[1 - core], nbuf.at[1 - core], sib_s, sib_r, sibling, r)
    out_pass_z()
    loads[1].wait()
    sib_in.wait_recv()

    def window_heads(quad):
        columns = w1[:, pl.ds(pl.multiple_of(quad * 768, 768), 768)]
        both = dot(nbuf[...].reshape(256, D), columns).astype(jnp.bfloat16)
        scores = []
        for h in range(4):
            at = h * 192
            mine = jnp.where(core == 0, both[:128, at : at + 64], both[128:, at : at + 64])
            scores.append(
                lax.dot_general(
                    mine, both[:, at + 64 : at + 128], NT, preferred_element_type=jnp.float32
                )
            )
        results = []
        for h in range(4):
            at = h * 192
            top = jnp.max(scores[h], axis=-1, keepdims=True)
            weights = jnp.exp2((scores[h] - top) * SCALE)
            total = jnp.sum(weights, axis=-1, keepdims=True)
            mixed = dot(weights.astype(jnp.bfloat16), both[:, at + 128 : at + 192])
            results.append(mixed / total)
        o1[:, pl.ds(pl.multiple_of(quad * 256, 256), 256)] = jnp.concatenate(
            results, axis=1
        ).astype(jnp.bfloat16)

    loop(0, 2, window_heads)
    pass_weights()
    loop(2, 4, window_heads)
    loads[2].wait()
    stream = x_ref[...] + dot(o1[...], wout[...])
    x_ref[...] = stream
    nall[x_at] = layer_norm(stream, gains[1:2])

    def tokens_at(x, part):
        if part == 2:
            return nall.at[x % 4]
        return nall.at[x % 4, pl.ds(part * 64, 64)]

    def tokens_x(step, part, x, number):
        at = tokens_at(x, part)
        return remote(
            at, at, ns.at[number], nr.at[part, x % 4], i, ((x_at + step) % 4) * 4 + z_at
        )

    def tokens_in(x, part):
        at = tokens_at(x, part)
        remote(at, at, ns.at[0], nr.at[part, x % 4], i, r).wait_recv()

    tokens_copies = [
        tokens_x(1, 2, x_at, 0),
        tokens_x(3, 2, x_at, 1),
        tokens_x(1, 0, x_at + 3, 2),
        tokens_x(3, 1, x_at + 1, 3),
    ]
    tokens_copies[0].start()
    tokens_copies[1].start()
    pass_weights_last()
    for k in range(1, 4):
        z = (z_at + k) % 4
        at = wqall.at[z, 1 - core]
        remote(at, at, qss.at[z], qsr.at[z], sibling, r).wait_recv()

    def to_head(x, k):
        quarter = (fourth + k) % 4
        at = q_out.at[x * 4 + quarter]
        return remote(
            at, q_in.at[x * 4 + fourth], as_.at[x * 4 + quarter], ar.at[x * 4 + fourth],
            member(quarter), r,
        )

    for step in (0, 1, 3, 2):
        x = (x_at + step) % 4
        if step == 1:
            tokens_in(x_at + 3, 2)
            tokens_copies[2].start()
            tokens_in(x_at + 1, 2)
            tokens_copies[3].start()
        elif step == 2:
            tokens_in(x_at + 2, 0)
            tokens_in(x_at + 2, 1)
        tokens = nall[x]
        for k in (1, 2, 3, 0):
            quarter = (fourth + k) % 4
            found = lax.dot_general(
                wqall[quarter].reshape(192, D), tokens, NT, preferred_element_type=jnp.float32
            ).astype(jnp.bfloat16)
            if k > 0:
                q_out[x * 4 + quarter] = found
                to_head(x, k).start()
            else:
                q_in[x * 4 + fourth] = found

    def head_in(x):
        for k in range(1, 4):
            s = x * 4 + (fourth + k) % 4
            remote(q_out.at[s], q_in.at[s], as_.at[s], ar.at[s], i, r).wait_recv()

    out_pass_x()
    loop(0, 4, head_in)
    for s in range(N):
        at = s * 128
        qt[:, at : at + 128] = q_in[s, 0:64]
        kb[at : at + 128, :] = q_in[s, 64:128].astype(jnp.float32).T.astype(jnp.bfloat16)
        vt[:, at : at + 128] = q_in[s, 128:192]

    def home(j):
        return remote(
            o_out.at[j], o_in.at[my_head], bs.at[j], br.at[my_head],
            member(j % 4), (j // 4) * 4 + z_at,
        )

    def attend(k):
        blocks = [(2 * k + e + my_head // 2 + 1) % 8 for e in range(2)]
        scores = [
            dot(kb[...], qt[:, pl.ds(pl.multiple_of(b * 256, 256), 256)]) for b in blocks
        ]
        for b, score in zip(blocks, scores):
            top = jnp.max(score, axis=0, keepdims=True)
            weights = jnp.exp2((score - top) * SCALE)
            total = jnp.sum(weights, axis=0, keepdims=True)
            mixed = (dot(vt[...], weights.astype(jnp.bfloat16)) / total).astype(jnp.bfloat16)
            for e in range(2):
                j = 2 * b + e
                o_out[j] = mixed[:, 128 * e : 128 * e + 128]

                @pl.when(j != my_head)
                def _(j=j):
                    home(j).start()

    loop(0, 4, attend)
    o_in[my_head] = o_out[my_head]
    out_last()

    def home_in(k):
        s = (my_head + k) % N
        remote(o_out.at[s], o_in.at[s], bs.at[s], br.at[s], i, r).wait_recv()

    loop(1, N, home_in)
    attended = o_in[...].reshape(D, 128).astype(jnp.float32).T.astype(jnp.bfloat16)
    stream = x_ref[...] + dot(attended, woall[...].reshape(D, D))
    loads[3].wait()
    logits = dot(layer_norm(stream, gains[2:3]), hw[...])
    lout[...] = logits.astype(jnp.bfloat16).reshape(8, 16, NCLS)

    collector = 2 * kc_mine + my_tile % 2

    def l1(k):
        return remote(
            lout.at[k], lin.at[my_tile // 2], l1s.at[k], l1r.at[my_tile // 2], collector, upper * 8 + k
        )

    def l1_start(k):
        away = (collector != i) | (upper * 8 + k != r)

        @pl.when(away)
        def _():
            l1(k).start()

        @pl.when(jnp.logical_not(away))
        def _():
            lin[my_tile // 2] = lout[k]

    loop(0, 8, l1_start)
    kc = i // 2

    def l1_in(k):
        giver, at = worker(2 * k + i % 2, r8, kc // 2, kc % 2)

        @pl.when((giver != i) | (at != r))
        def _():
            remote(lout.at[0], lin.at[k], l1s.at[0], l1r.at[k], i, r).wait_recv()

    slot = [owners[t] * MOST + ranks[t] for t in range(N)]
    lane = lax.broadcasted_iota(jnp.int32, (N * MOST * 16, 128), 1)
    line = lax.broadcasted_iota(jnp.int32, (N * MOST * 16, 128), 0)
    wanted = jnp.zeros((N * MOST * 16, 128), jnp.int32)
    for k in range(8):
        wanted = jnp.where(
            lane // 16 == k, jnp.where(core == 0, slot[2 * k], slot[2 * k + 1]), wanted
        )
    route = jnp.where(line == wanted * 16 + lane % 16, 1.0, 0.0).astype(jnp.bfloat16)
    loop(0, 8, l1_in)
    rout[...] = (
        dot(route, lin[...].reshape(128, NCLS)).astype(jnp.bfloat16).reshape(N, MOST, 16, NCLS)
    )

    def l2(s):
        return remote(rout.at[s], rin.at[i], l2s.at[s], l2r.at[i], s, r)

    loop(1, N, lambda k: l2((i + k) % N).start())
    rin[i] = rout[i]

    cell = lax.broadcasted_iota(jnp.int32, (2 * SC, 128), 0)
    token = lax.broadcasted_iota(jnp.int32, (2 * SC, 128), 1)
    t_row = (token // 8) % 2
    t_col = (token // 16) * 8 + token % 8
    c_row = jnp.where(cell >= SC, 1, 0)
    c_col = cell - SC * c_row
    count = jnp.zeros((2 * SC, 128), jnp.float32)
    spots = []
    for m in range(MOST):
        chosen = (c_row == t_row) & (c_col == t_col + begin[m])
        spots.append(jnp.where(chosen, 1.0, 0.0).astype(jnp.bfloat16))
        count = count + jnp.where((c_col >= begin[m]) & (c_col < begin[m] + 64), 1.0, 0.0)

    def l2_in(k):
        s = (i + k) % N
        remote(rout.at[s], rin.at[s], l2s.at[s], l2r.at[s], s, r).wait_recv()

    loop(1, N, l2_in)
    total = jnp.zeros((2 * SC, NCLS), jnp.float32)
    for m in range(MOST):
        pieces = [rin[2 * k, m] + rin[2 * k + 1, m] for k in range(8)]
        total = total + dot(spots[m], jnp.concatenate(pieces, axis=0))
    out_ref[...] = (total / jnp.maximum(count, 1.0)).reshape(2, SC, NCLS)

    loop(1, N, lambda k: p1((i + k) % N).wait_send())

    loop(0, 8, pos_sent)
    loop(1, N, lambda k: p2((my_tile + k) % N).wait_send())

    @pl.when(away)
    def _():
        p2(my_tile).wait_send()

    sib.wait_send()
    for k in range(1, 4):
        weights_sibling(k).wait_send()
    for copy in weights_copies + tokens_copies:
        copy.wait_send()
    out_sent()

    def heads_sent(x):
        for k in range(1, 4):
            to_head(x, k).wait_send()

    loop(0, 4, heads_sent)
    loop(1, N, lambda k: home((my_head + k) % N).wait_send())

    def l1_sent(k):
        @pl.when((collector != i) | (upper * 8 + k != r))
        def _():
            l1(k).wait_send()

    loop(0, 8, l1_sent)
    loop(1, N, lambda k: l2((i + k) % N).wait_send())


def local(
    scene_band, tile_list, embed_weight, position, norm_gains, window_qkv, window_out,
    global_qkv, global_out, head_weight,
):
    core = lax.axis_index("tile") % 2
    parts = position.reshape(2, 4, 2, 8, D)
    pos = lax.dynamic_index_in_dim(parts, core, 2, False).transpose(1, 0, 2, 3).reshape(4, 16, D)
    wq = global_qkv.T.reshape(2, 96, D)
    wo = global_out.reshape(2, 32, D)
    bf = jnp.bfloat16
    vmem = pl.BlockSpec(memory_space=pltpu.VMEM)
    hbm = pl.BlockSpec(memory_space=pl.ANY)
    dma = pltpu.SemaphoreType.DMA
    return pl.pallas_call(
        kernel,
        out_shape=jax.ShapeDtypeStruct((2, SC, NCLS), jnp.float32),
        in_specs=[hbm] + [vmem] * 5 + [hbm] * 4,
        out_specs=vmem,
        scratch_shapes=[
            pltpu.SMEM((3, N), jnp.int32),
            pltpu.VMEM((PV, D), bf),
            pltpu.VMEM((D, 3 * D), bf),
            pltpu.VMEM((D, D), bf),
            pltpu.VMEM((D, NCLS), bf),
            dma((5,)),
            pltpu.VMEM((N, MOST, 16, FH), bf),
            pltpu.VMEM((N, MOST, 16, FH), bf),
            pltpu.VMEM((N, 16, FH), bf),
            pltpu.VMEM((2, 8, 16, FH), bf),
            pltpu.VMEM((8, 16, D), bf),
            pltpu.VMEM((2, 128, D), bf),
            pltpu.VMEM((128, D), jnp.float32),
            pltpu.VMEM((128, D), bf),
            pltpu.VMEM((4, 2, 96, D), bf),
            pltpu.VMEM((N, 2, 32, D), bf),
            pltpu.VMEM((N, 192, 128), bf),
            pltpu.VMEM((N, 192, 128), bf),
            pltpu.VMEM((64, 2048), bf),
            pltpu.VMEM((2048, 64), bf),
            pltpu.VMEM((64, 2048), bf),
            pltpu.VMEM((N, 64, 128), bf),
            pltpu.VMEM((N, 64, 128), bf),
            pltpu.VMEM((8, 16, NCLS), bf),
            pltpu.VMEM((8, 16, NCLS), bf),
            pltpu.VMEM((N, MOST, 16, NCLS), bf),
            pltpu.VMEM((N, MOST, 16, NCLS), bf),
            pltpu.VMEM((4, 128, D), bf),
            pltpu.SemaphoreType.REGULAR,
            dma((4,)), dma((3, 4)),
            dma((N,)), dma((N,)), dma((N,)), dma((N,)), dma((8,)), dma((8,)), dma, dma,
            dma((4,)), dma((4,)), dma((3, 4)), dma((4,)),
            dma((3,)), dma((3,)), dma((3,)), dma((3,)), dma((4,)), dma((4,)), dma((4,)), dma((4,)),
            dma((N,)), dma((N,)), dma((N,)), dma((N,)), dma((8,)), dma((8,)), dma((N,)), dma((N,)),
        ],
        compiler_params=pltpu.CompilerParams(
            collective_id=0, has_side_effects=True, vmem_limit_bytes=56 * 1024 * 1024
        ),
    )(
        tile_list.T, scene_band, pos, wq, wo, norm_gains,
        embed_weight, window_qkv, window_out, head_weight,
    )


def solution(mesh):
    return jax.shard_map(
        local,
        mesh=mesh,
        in_specs=(
            P("seq", "tile", None), P(), P(), P("seq", None), P(), P(), P(),
            P(None, "seq"), P("seq", None), P(),
        ),
        out_specs=P("seq", "tile", None),
        check_vma=False,
    )
```
